256 devices in a mesh: pp: 4 (over y), node: 8 (over x, core), local: 8 (over z).
Axes of the slice: x: 4, y: 4, z: 8, core: 2. Of those that a mesh axis runs over, the one named last changes fastest.
Arguments:
- act_fwd: bfloat16 [4, 8192, 4096], P('pp', ('node', 'local')), may hold values from -6 to 6
- routes_fwd: int32 [4, 8192, 1], P('pp', ('node', 'local')), may hold values from 0 to 7; in each aligned block of 128 rows (0 to 127, 128 to 255, ..., all dimensions but the last counted through in order) at most 20 rows name the same one
- weight_fwd: float32 [4, 8192], P('pp', ('node', 'local')), may hold values from 0.25 to 1
- grad_bwd: bfloat16 [4, 8192, 4096], P('pp', ('node', 'local')), may hold values from -6 to 6
- routes_bwd: int32 [4, 8192, 1], P('pp', ('node', 'local')), may hold values from 0 to 7; in each aligned block of 128 rows (0 to 127, 128 to 255, ..., all dimensions but the last counted through in order) at most 20 rows name the same one
- weight_bwd: float32 [4, 8192], P('pp', ('node', 'local')), may hold values from 0.25 to 1
- saved_bwd: bfloat16 [4, 8192, 2048], P('pp', ('node', 'local')), may hold values from -8 to 8
- w_gate_up: bfloat16 [4, 8, 4096, 2048], P('pp', 'node', 'local'), may hold values from -0.09375 to 0.09375
- w_down: bfloat16 [4, 8, 1024, 4096], P('pp', 'node', None, 'local'), may hold values from -0.1875 to 0.1875
Outputs:
- next_input: bfloat16 [4, 8192, 4096], P('pp', ('node', 'local'))
- prev_grad: bfloat16 [4, 8192, 4096], P('pp', ('node', 'local'))
The draws below stay inside these ranges and needn't reach their ends.
Inputs may be any that keep to these rules, and one draw needn't show every extreme that they name: `routes_fwd`: within each device's 128 tokens (aligned blocks of rows), no expert is named more than 20 times, a bound that some block reaches. `routes_bwd`: within each device's 128 tokens (aligned blocks of rows), no expert is named more than 20 times, a bound that some block reaches.
All inputs are finite; a program needn't handle non-finite values.
Results may differ from the reference program's by a relative error of at most 0.017.
Values may be sent and summed in bfloat16 or wider, within the bound.
A program may use at most 128 MiB of HBM per device.

```python
import math
import jax
import jax.numpy as jnp
import numpy as np
from jax import lax

D = 4096
H = 1024
TOK_DEV = 128
TOPK = 1
EXPERTS = 8
CAP = 20
TOKENS = 8192
N_PP = 4
N_NODE = 8
N_LOCAL = 8


def levels(own_key, dims, shards, low, top_value):
    factor_of = 1.0
    for dim, parts in shards:
        draws = jax.random.uniform(jax.random.fold_in(jax.random.fold_in(own_key, 6), dim), (parts,), jnp.float32, low / len(shards), top_value / len(shards))
        factor_of = factor_of * jnp.repeat(jnp.exp(draws), dims[dim] // parts).reshape((-1,) + (1,) * (len(dims) - 1 - dim))
    return factor_of


def assign_block(stream_key, own, number, rows, count, top, reach, skew):
    order = jax.random.permutation(stream_key, count)
    packed, common = load_shares(count, rows * top, reach, skew, True), load_shares(count, rows * top, reach, skew, False)
    places = jnp.arange(count)

    def named(sizes, turn):
        used = int((sizes > 0).sum())
        fixed = max(1, used // 4)
        passed = fixed + (places - fixed + turn * (used - fixed)) % max(1, count - fixed)
        return jnp.zeros((count,), jnp.int32).at[order[jnp.where(places < fixed, places, passed)]].set(jnp.asarray(sizes, jnp.int32))

    sizes = jnp.where(number % 4 == 0, named(packed, number // 4), named(common, number - number // 4 - 1))
    mixed = jax.random.permutation(jax.random.fold_in(own, 3), count)
    source_of, sink = mixed[0:count // 2 * 2:2], mixed[1:count // 2 * 2:2]
    room = jnp.minimum(sizes[source_of] - 1, reach - sizes[sink]) // 2
    room = jnp.where((source_of == order[0]) | (sink == order[0]) | (sizes[sink] == 0), 0, jnp.maximum(room, 0))
    passed = jax.random.randint(jax.random.fold_in(own, 4), (count // 2,), 0, 1 << 20) % (room + 1)
    sizes = sizes.at[source_of].add(-passed).at[sink].add(passed)
    items = jnp.searchsorted(jnp.cumsum(sizes), jnp.arange(rows * top), side="right").astype(jnp.int32)
    listing = items.reshape(top, rows).T
    listing = listing[jax.random.permutation(jax.random.fold_in(own, 1), rows)]
    turn = jax.random.randint(jax.random.fold_in(own, 2), (rows, 1), 0, top)
    return jnp.take_along_axis(listing, (jnp.arange(top)[None, :] + turn) % top, axis=1)


def load_shares(amount, total, limit, lean, full):
    portions = [(1 << 20) // math.isqrt(standing ** lean) + 1 for standing in range(1, amount + 1)]
    largest = limit if full else min(limit, max(-(-total // amount), total * portions[0] // sum(portions)))
    least = 1 if total - largest >= amount - 1 else 0
    given, spare = [largest] + [least] * (amount - 1), total - largest - least * (amount - 1)
    while spare > 0:
        free = [i for i in range(1, amount) if given[i] < largest] or [i for i in range(1, amount) if given[i] < limit]
        pool, remaining = sum([portions[i] for i in free]), spare
        for i in free:
            extra = min(limit - given[i], max(1, remaining * portions[i] // pool), spare)
            given[i] = given[i] + extra
            spare = spare - extra
    return np.array(given)


def gaussian(rng, dims, spread, limit, pieces=(), held_as=jnp.bfloat16):
    gain = levels(rng, dims, pieces, -0.22, 0.18) if pieces else 1.0
    drawn = jax.random.normal(rng, dims, jnp.float32) * spread * gain
    return jnp.minimum(jnp.maximum(drawn, -limit), limit).astype(held_as)


def setup_inputs(seed: int = 0) -> dict:
    splits = jax.random.split(jax.random.key(seed), 10)
    act_fwd = gaussian(splits[0], (N_PP, TOKENS, D), 1.0, 6.0, ((0, 4), (1, 64)))
    routes_fwd_keys = jax.random.split(jax.random.fold_in(splits[1], 1), N_PP * TOKENS // TOK_DEV)
    routes_fwd_turns = jax.random.permutation(jax.random.fold_in(splits[1], 3), N_PP * TOKENS // TOK_DEV)
    routes_fwd = jax.vmap(lambda own, number: assign_block(jax.random.fold_in(splits[1], 2), own, number, TOK_DEV, EXPERTS, TOPK, CAP, 2))(routes_fwd_keys, routes_fwd_turns).reshape((N_PP, TOKENS, TOPK))
    weight_fwd = jnp.clip(jnp.exp(math.log(1.0) - 1.3862944 * jax.random.uniform(splits[2], (N_PP, TOKENS), jnp.float32) ** levels(splits[2], (N_PP, TOKENS), ((0, 4), (1, 64)), -0.2, 0.2)), 0.25, 1.0)
    grad_bwd = gaussian(splits[3], (N_PP, TOKENS, D), 1.0, 6.0, ((0, 4), (1, 64)))
    routes_bwd_keys = jax.random.split(jax.random.fold_in(splits[4], 1), N_PP * TOKENS // TOK_DEV)
    routes_bwd_turns = jax.random.permutation(jax.random.fold_in(splits[4], 3), N_PP * TOKENS // TOK_DEV)
    routes_bwd = jax.vmap(lambda own, number: assign_block(jax.random.fold_in(splits[4], 2), own, number, TOK_DEV, EXPERTS, TOPK, CAP, 2))(routes_bwd_keys, routes_bwd_turns).reshape((N_PP, TOKENS, TOPK))
    weight_bwd = jnp.clip(jnp.exp(math.log(1.0) - 1.3862944 * jax.random.uniform(splits[5], (N_PP, TOKENS), jnp.float32) ** levels(splits[5], (N_PP, TOKENS), ((0, 4), (1, 64)), -0.2, 0.2)), 0.25, 1.0)
    saved_bwd = gaussian(splits[6], (N_PP, TOKENS, 2 * H), 1.5, 8.0, ((0, 4), (1, 64)))
    w_gate_up = gaussian(splits[7], (N_PP, EXPERTS, D, 2 * H), D ** -0.5, 0.09375, ((0, 4), (1, 8), (2, 8)))
    w_down = gaussian(splits[8], (N_PP, EXPERTS, H, D), H ** -0.5, 0.1875, ((0, 4), (1, 8), (3, 8)))
    return {"act_fwd": act_fwd, "routes_fwd": routes_fwd, "weight_fwd": weight_fwd, "grad_bwd": grad_bwd, "routes_bwd": routes_bwd, "weight_bwd": weight_bwd, "saved_bwd": saved_bwd, "w_gate_up": w_gate_up, "w_down": w_down}


def route_slots(route):
    device_count = N_NODE * N_LOCAL
    blocked = route.reshape(device_count, TOK_DEV).astype(jnp.int32)
    onehot = (blocked[:, :, None] == jnp.arange(EXPERTS, dtype=jnp.int32)[None, None, :]).astype(jnp.int32)
    before = jnp.cumsum(onehot, axis=1) - onehot
    slot_of = jnp.sum(before * onehot, axis=2).astype(jnp.int32)
    device_of = jnp.broadcast_to(jnp.arange(device_count, dtype=jnp.int32)[:, None], (device_count, TOK_DEV))
    return blocked.reshape(-1), device_of.reshape(-1), slot_of.reshape(-1)


def pack_rows(values, where):
    expert_of, device_of, slot_of = where
    buffer = jnp.zeros((EXPERTS, N_NODE * N_LOCAL, CAP, values.shape[1]), values.dtype)
    buffer = buffer.at[expert_of, device_of, slot_of].set(values)
    return buffer.reshape(EXPERTS, N_NODE * N_LOCAL * CAP, values.shape[1])


def unpack_rows(rows_out, where):
    expert_of, device_of, slot_of = where
    blocked = rows_out.reshape(EXPERTS, N_NODE * N_LOCAL, CAP, rows_out.shape[-1])
    return blocked[expert_of, device_of, slot_of]


def block_sum(left, right):
    row_count = left.shape[0]
    column = left.shape[1] // N_LOCAL
    left_blocks = left.astype(jnp.float32).reshape(row_count, N_LOCAL, column)
    right_blocks = right.astype(jnp.float32).reshape(N_LOCAL, column, right.shape[1])
    partial_value = jnp.einsum("rjd,jdk->rjk", left_blocks, right_blocks)
    return jnp.sum(partial_value.astype(jnp.bfloat16).astype(jnp.float32), axis=1)


def expert_forward(operands):
    rows_in, w_gu, w_dn = operands
    preact = block_sum(rows_in, w_gu)
    hidden = (jax.nn.silu(preact[:, :H]) * preact[:, H:]).astype(jnp.bfloat16)
    return jnp.dot(hidden, w_dn, preferred_element_type=jnp.float32).astype(jnp.bfloat16)


def expert_backward(operands):
    rows_in, saved_rows, w_gu, w_dn = operands
    grad_hidden = block_sum(rows_in, jnp.transpose(w_dn))
    gate_pre = saved_rows[:, :H].astype(jnp.float32)
    up_pre = saved_rows[:, H:].astype(jnp.float32)
    sigmoid_g = 1.0 / (1.0 + jnp.exp(-gate_pre))
    grad_gate = grad_hidden * up_pre * sigmoid_g * (1.0 + gate_pre * (1.0 - sigmoid_g))
    grad_up = grad_hidden * gate_pre * sigmoid_g
    grad_gu = jnp.concatenate([grad_gate, grad_up], axis=1).astype(jnp.bfloat16)
    return jnp.dot(grad_gu, jnp.transpose(w_gu), preferred_element_type=jnp.float32).astype(jnp.bfloat16)


def reference(act_fwd, routes_fwd, weight_fwd, grad_bwd, routes_bwd, weight_bwd, saved_bwd, w_gate_up, w_down):
    outputs_fwd = []
    outputs_bwd = []
    for segment in range(N_PP):
        where_a = route_slots(routes_fwd[segment, :, 0])
        tokens_a = act_fwd[segment]
        rows_a = pack_rows(tokens_a, where_a)
        done_a = lax.map(expert_forward, (rows_a, w_gate_up[segment], w_down[segment]))
        moe_a = unpack_rows(done_a, where_a)
        result_a = tokens_a.astype(jnp.float32) + weight_fwd[segment][:, None] * moe_a.astype(jnp.float32)
        outputs_fwd.append(result_a.astype(jnp.bfloat16))

        where_b = route_slots(routes_bwd[segment, :, 0])
        cotangent = grad_bwd[segment]
        scaled = (weight_bwd[segment][:, None] * cotangent.astype(jnp.float32)).astype(jnp.bfloat16)
        rows_b = pack_rows(scaled, where_b)
        saved_b = pack_rows(saved_bwd[segment], where_b)
        done_b = lax.map(expert_backward, (rows_b, saved_b, w_gate_up[segment], w_down[segment]))
        moe_b = unpack_rows(done_b, where_b)
        result_b = cotangent.astype(jnp.float32) + moe_b.astype(jnp.float32)
        outputs_bwd.append(result_b.astype(jnp.bfloat16))
    next_input = jnp.roll(jnp.stack(outputs_fwd, axis=0), 1, axis=0)
    prev_grad = jnp.roll(jnp.stack(outputs_bwd, axis=0), -1, axis=0)
    return (next_input, prev_grad)
```

```python
import jax
import jax.numpy as jnp
from jax import lax
from jax.sharding import PartitionSpec as P


def place_matrix(route, expert_count, capacity):
    rows = route.shape[0]
    same = route[:, None] == route[None, :]
    earlier = jnp.arange(rows, dtype=jnp.int32)[None, :] < jnp.arange(rows, dtype=jnp.int32)[:, None]
    slot_index = jnp.sum((same & earlier).astype(jnp.int32), axis=1)
    target = route * capacity + slot_index
    positions = jnp.arange(expert_count * capacity, dtype=jnp.int32)
    return (positions[:, None] == target[None, :]).astype(jnp.bfloat16)


def pack_rows(placer, values):
    return jnp.dot(placer, values, preferred_element_type=jnp.float32).astype(jnp.bfloat16)


def unpack_rows(placer, packed):
    return lax.dot_general(
        placer, packed, (((0,), (0,)), ((), ())), preferred_element_type=jnp.float32
    )


def swap(packed, nodes):
    blocks = packed.reshape(nodes, -1, packed.shape[1])
    return lax.all_to_all(blocks, "node", split_axis=0, concat_axis=0, tiled=True).reshape(packed.shape)


def body(
    act_fwd, routes_fwd, weight_fwd, grad_bwd, routes_bwd, weight_bwd, saved_bwd, w_gate_up, w_down
):
    nodes = lax.axis_size("node")
    capacity = 5 * act_fwd.shape[1] // (4 * nodes)
    w_gu = lax.all_gather(w_gate_up[0, 0], "local", axis=0, tiled=True)
    w_dn = lax.all_gather(w_down[0, 0], "local", axis=0, tiled=False)
    shards, hidden_units, column = w_dn.shape
    tokens = act_fwd[0]
    cotangent = grad_bwd[0]
    placer_a = place_matrix(routes_fwd[0, :, 0], nodes, capacity)
    placer_b = place_matrix(routes_bwd[0, :, 0], nodes, capacity)
    scaled = (weight_bwd[0][:, None] * cotangent.astype(jnp.float32)).astype(jnp.bfloat16)
    rows_a = swap(pack_rows(placer_a, tokens), nodes)
    rows_b = swap(pack_rows(placer_b, scaled), nodes)
    saved = swap(pack_rows(placer_b, saved_bwd[0]), nodes)
    grad_hidden = sum(
        lax.dot_general(
            rows_b[:, j * column : (j + 1) * column], w_dn[j], (((1,), (1,)), ((), ())),
            preferred_element_type=jnp.float32,
        )
        for j in range(shards)
    )
    gate_pre = saved[:, :hidden_units].astype(jnp.float32)
    up_pre = saved[:, hidden_units:].astype(jnp.float32)
    sigmoid_g = 1.0 / (1.0 + jnp.exp(-gate_pre))
    grad_gate = grad_hidden * up_pre * sigmoid_g * (1.0 + gate_pre * (1.0 - sigmoid_g))
    grad_up = grad_hidden * gate_pre * sigmoid_g
    grad_gu = jnp.concatenate([grad_gate, grad_up], axis=1).astype(jnp.bfloat16)
    done_b = lax.dot_general(
        grad_gu, w_gu, (((1,), (1,)), ((), ())), preferred_element_type=jnp.float32
    ).astype(jnp.bfloat16)
    preact = jnp.dot(rows_a, w_gu, preferred_element_type=jnp.float32)
    hidden = (jax.nn.silu(preact[:, :hidden_units]) * preact[:, hidden_units:]).astype(jnp.bfloat16)
    done_a = jnp.concatenate(
        [jnp.dot(hidden, w_dn[j], preferred_element_type=jnp.float32).astype(jnp.bfloat16) for j in range(shards)],
        axis=1,
    )
    moe_a = unpack_rows(placer_a, swap(done_a, nodes))
    moe_b = unpack_rows(placer_b, swap(done_b, nodes))
    result_a = (tokens.astype(jnp.float32) + weight_fwd[0][:, None] * moe_a).astype(jnp.bfloat16)
    result_b = (cotangent.astype(jnp.float32) + moe_b).astype(jnp.bfloat16)
    length = lax.axis_size("pp")
    next_input = lax.ppermute(result_a[None], "pp", [(i, (i + 1) % length) for i in range(length)])
    prev_grad = lax.ppermute(result_b[None], "pp", [(i, (i - 1) % length) for i in range(length)])
    return (next_input, prev_grad)


def solution(mesh):
    in_specs = (
        P("pp", ("node", "local"), None),
        P("pp", ("node", "local"), None),
        P("pp", ("node", "local")),
        P("pp", ("node", "local"), None),
        P("pp", ("node", "local"), None),
        P("pp", ("node", "local")),
        P("pp", ("node", "local"), None),
        P("pp", "node", "local", None),
        P("pp", "node", None, "local"),
    )
    out_specs = (P("pp", ("node", "local"), None), P("pp", ("node", "local"), None))
    return jax.shard_map(body, mesh=mesh, in_specs=in_specs, out_specs=out_specs, check_vma=False)
```

```python
import functools

import jax
import jax.numpy as jnp
from jax import lax
from jax.experimental import pallas as pl
from jax.experimental.pallas import tpu as pltpu
from jax.sharding import PartitionSpec as P

MESH = pl.DeviceIdType.MESH
ROWS = 32
NT = (((1,), (1,)), ((), ()))


def kernel(
    act, route_a, weight_a, grad, route_b, weight_b, saved, w_gu, w_dn,
    out_a, out_b,
    act_v, grad_v, saved_v, gu_v, dn_v, xs_a, xr_a, xs_b, xr_b, ss, sr, back_a, back_b, res_a, res_b,
    pre, dh, dgu, hid, pick_a, pick_b, scale_a,
    load_sem, disp_send, disp_recv, dn_send, dn_recv, gu_send, gu_recv,
    ret_a_send, ret_a_recv, ret_b_send, ret_b_recv, relay_send, relay_recv,
):
    n_pp, n_node, n_local = lax.axis_size("pp"), lax.axis_size("node"), lax.axis_size("local")
    pp, node, me = lax.axis_index("pp"), lax.axis_index("node"), lax.axis_index("local")
    tokens, features = act.shape
    hidden = w_dn.shape[0]
    column = w_dn.shape[1]
    total = n_node * ROWS
    half = n_local // 2

    def wrap(index, size):
        return lax.rem(index + size, size)

    right, left = wrap(me + 1, n_local), wrap(me - 1, n_local)
    ahead, behind = wrap(pp + 1, n_pp), wrap(pp - 1, n_pp)
    peers = [wrap(node + k, n_node) for k in range(1, n_node)]

    loads = [
        pltpu.make_async_copy(grad, grad_v, load_sem.at[0]),
        pltpu.make_async_copy(saved, saved_v, load_sem.at[1]),
        pltpu.make_async_copy(act, act_v, load_sem.at[2]),
        pltpu.make_async_copy(w_dn, dn_v.at[me], load_sem.at[3]),
        pltpu.make_async_copy(w_gu, gu_v.at[me], load_sem.at[4]),
    ]

    barrier = pltpu.get_barrier_semaphore()
    for peer in peers:
        pl.semaphore_signal(barrier, inc=1, device_id={"node": peer}, device_id_type=MESH)
    for neighbour in (left, right):
        pl.semaphore_signal(barrier, inc=1, device_id={"local": neighbour}, device_id_type=MESH)
    for neighbour in (behind, ahead):
        pl.semaphore_signal(barrier, inc=1, device_id={"pp": neighbour}, device_id_type=MESH)
    for load in loads:
        load.start()
    pl.semaphore_wait(barrier, n_node - 1 + 4)

    def hop(buffer, send, recv, way, far, chunk, source=None):
        owner = wrap(me - far, n_local) if way == 0 else wrap(me + far, n_local)
        size = buffer.shape[1] // 2
        here = buffer.at[owner, pl.ds(chunk * size, size), :]
        slot = (way * half + far) * 2 + chunk
        return pltpu.make_async_remote_copy(
            src_ref=here if source is None else source.at[pl.ds(chunk * size, size), :],
            dst_ref=here,
            send_sem=send.at[slot],
            recv_sem=recv.at[slot],
            device_id={"local": right if way == 0 else left},
            device_id_type=MESH,
        )

    def landed(buffer, send, recv, way, far, chunk):
        owner = wrap(me - far, n_local) if way == 0 else wrap(me + far, n_local)
        size = buffer.shape[1] // 2
        here = buffer.at[owner, pl.ds(chunk * size, size), :]
        slot = (way * half + far - 1) * 2 + chunk
        return pltpu.make_async_remote_copy(
            src_ref=here, dst_ref=here, send_sem=send.at[slot], recv_sem=recv.at[slot],
            device_id={"local": right if way == 0 else left}, device_id_type=MESH,
        )

    dn = (dn_v, dn_send, dn_recv)
    gu = (gu_v, gu_send, gu_recv)

    def ring_start(ring, source):
        for chunk in range(2):
            for way in range(2):
                hop(*ring, way, 0, chunk, source).start()

    def ring_step(ring, far):
        for chunk in range(2):
            for way in range(2):
                landed(*ring, way, far, chunk).wait_recv()
                if chunk == way:
                    hop(*ring, way, far, chunk).start()
                else:
                    @pl.when(far < half - 1)
                    def _():
                        hop(*ring, way, far, chunk).start()

    def ring_last(ring):
        for way in range(2):
            landed(*ring, way, half, way).wait_recv()

    def ring_drain(ring):
        for far in range(half):
            for chunk in range(2):
                for way in range(2):
                    if far < half - 1 or chunk == way:
                        hop(*ring, way, far, chunk).wait_send()

    ring_start(dn, w_dn)

    def places(route_ref):
        route = jnp.broadcast_to(route_ref[...].astype(jnp.float32), (tokens, tokens))
        turned = jnp.transpose(route)
        first = lax.broadcasted_iota(jnp.int32, (tokens, tokens), 0)
        second = lax.broadcasted_iota(jnp.int32, (tokens, tokens), 1)
        same = route == turned
        slot_row = jnp.sum(jnp.where(same & (first < second), 1.0, 0.0), axis=0, keepdims=True)
        slot_col = jnp.sum(jnp.where(same & (second < first), 1.0, 0.0), axis=1, keepdims=True)
        row = route[0:1, :] * float(ROWS) + slot_row
        col = turned[:, 0:1] * float(ROWS) + slot_col
        put = lax.broadcasted_iota(jnp.int32, (total, tokens), 0).astype(jnp.float32) == row
        pick = lax.broadcasted_iota(jnp.int32, (tokens, total), 1).astype(jnp.float32) == col
        one, zero = jnp.float32(1), jnp.float32(0)
        return (
            jnp.where(put, one, zero).astype(jnp.bfloat16),
            jnp.where(pick, one, zero).astype(jnp.bfloat16),
        )

    def spread(weight_ref):
        turned = jnp.transpose(jnp.broadcast_to(weight_ref[...], (tokens, tokens)))
        return jnp.concatenate([turned] * (column // tokens), axis=1)

    def cols(block, width=None):
        width = column if width is None else width
        return pl.ds(pl.multiple_of(block * width, width), width)

    def at_node(index):
        return pl.ds(pl.multiple_of(index * ROWS, ROWS), ROWS)

    def dispatch(source, target, slot):
        for peer in peers:
            pltpu.make_async_remote_copy(
                src_ref=source.at[at_node(peer), :],
                dst_ref=target.at[at_node(node), :],
                send_sem=disp_send.at[slot],
                recv_sem=disp_recv.at[slot],
                device_id={"node": peer},
                device_id_type=MESH,
            ).start()
        target[at_node(node), :] = source[at_node(node), :]

    others = total - ROWS

    def all_of(buffer, sem, columns=slice(None)):
        part = buffer.at[pl.ds(0, others), columns]
        return pltpu.make_async_copy(part, part, sem)

    put_b, pick = places(route_b)
    pick_b[...] = pick
    scale_b = spread(weight_b)
    loads[0].wait()

    for block in range(features // column):
        at = slice(block * column, (block + 1) * column)
        scaled = (scale_b * grad_v[:, at].astype(jnp.float32)).astype(jnp.bfloat16)
        xs_b[:, at] = jnp.dot(put_b, scaled, preferred_element_type=jnp.float32).astype(jnp.bfloat16)
    dispatch(xs_b, xr_b, 0)
    loads[1].wait()
    for block in range(2 * hidden // column):
        at = slice(block * column, (block + 1) * column)
        ss[:, at] = jnp.dot(put_b, saved_v[:, at], preferred_element_type=jnp.float32).astype(jnp.bfloat16)
    dispatch(ss, sr, 1)
    put_a, pick = places(route_a)
    pick_a[...] = pick
    scale_a[...] = spread(weight_a)
    loads[2].wait()
    for block in range(features // column):
        at = slice(block * column, (block + 1) * column)
        xs_a[:, at] = jnp.dot(put_a, act_v[:, at], preferred_element_type=jnp.float32).astype(jnp.bfloat16)
    dispatch(xs_a, xr_a, 2)

    ring_step(dn, 1)
    ring_step(dn, 2)
    ring_start(gu, w_gu)
    ring_step(dn, 3)
    ring_last(dn)
    loads[3].wait()
    all_of(xr_b, disp_recv.at[0]).wait()

    dh[...] = jnp.zeros_like(dh)

    @pl.loop(0, n_local)
    def _(block):
        dh[...] += lax.dot_general(
            xr_b[:, cols(block)], dn_v[block], NT, preferred_element_type=jnp.float32
        )

    all_of(sr, disp_recv.at[1]).wait()

    part = 256

    @pl.loop(0, hidden // part)
    def _(index):
        at = cols(index, part)
        up_at = pl.ds(pl.multiple_of(hidden + index * part, part), part)
        gate = sr[:, at].astype(jnp.float32)
        up = sr[:, up_at].astype(jnp.float32)
        grad_h = dh[:, at]
        sigmoid = 1.0 / (1.0 + jnp.exp(-gate))
        dgu[:, at] = (grad_h * up * sigmoid * (1.0 + gate * (1.0 - sigmoid))).astype(jnp.bfloat16)
        dgu[:, up_at] = (grad_h * gate * sigmoid).astype(jnp.bfloat16)

    for slot, buffer in ((0, xs_b), (1, ss), (2, xs_a)):
        all_of(buffer, disp_send.at[slot]).wait()
    all_of(xr_a, disp_recv.at[2]).wait()
    pre[...] = jnp.zeros_like(pre)

    def forward(block):
        x = xr_a[:, cols(block)]

        @pl.loop(0, 2 * hidden // 512)
        def _(index):
            at = cols(index, 512)
            pre[:, at] += jnp.dot(x, gu_v[block, :, at], preferred_element_type=jnp.float32)

    def give_back(source, target, send, recv, block):
        for peer in peers:
            pltpu.make_async_remote_copy(
                src_ref=source.at[at_node(peer), cols(block)],
                dst_ref=target.at[at_node(node), cols(block)],
                send_sem=send.at[block],
                recv_sem=recv.at[block],
                device_id={"node": peer},
                device_id_type=MESH,
            ).start()
        target[at_node(node), cols(block)] = source[at_node(node), cols(block)]

    def backward(block):
        xs_b[:, cols(block)] = lax.dot_general(
            dgu[...], gu_v[block], NT, preferred_element_type=jnp.float32
        ).astype(jnp.bfloat16)
        give_back(xs_b, back_b, ret_b_send, ret_b_recv, block)

    def relay(source, target, slot, to, block):
        return pltpu.make_async_remote_copy(
            src_ref=source.at[:, cols(block)],
            dst_ref=target.at[:, cols(block)],
            send_sem=relay_send.at[slot],
            recv_sem=relay_recv.at[slot],
            device_id={"pp": to},
            device_id_type=MESH,
        )

    def finish_b(block):
        all_of(back_b, ret_b_recv.at[block], cols(block)).wait()
        moe = jnp.dot(pick_b[...], back_b[:, cols(block)], preferred_element_type=jnp.float32)
        res_b[:, cols(block)] = (grad_v[:, cols(block)].astype(jnp.float32) + moe).astype(jnp.bfloat16)
        relay(res_b, out_b, 1, behind, block).start()

    def finish_a(block):
        all_of(back_a, ret_a_recv.at[block], cols(block)).wait()
        moe = jnp.dot(pick_a[...], back_a[:, cols(block)], preferred_element_type=jnp.float32)
        res_a[:, cols(block)] = (
            act_v[:, cols(block)].astype(jnp.float32) + scale_a[...] * moe
        ).astype(jnp.bfloat16)
        relay(res_a, out_a, 0, ahead, block).start()

    def block_at(turn):
        far = (turn + 1) // 2
        return wrap(me + jnp.where(turn % 2 == 1, -far, far), n_local)

    loads[4].wait()

    @pl.loop(0, half)
    def _(far):
        @pl.when(far > 0)
        def _():
            ring_step(gu, far)

        @pl.loop(jnp.maximum(2 * far - 1, 0), 2 * far + 1)
        def _(turn):
            forward(block_at(turn))
            backward(block_at(turn))

        @pl.when(far > 0)
        def _():
            @pl.loop(jnp.maximum(2 * far - 3, 0), 2 * far - 1)
            def _(turn):
                finish_b(block_at(turn))

    ring_last(gu)
    final = wrap(me + half, n_local)
    forward(final)

    @pl.loop(0, hidden // part)
    def _(index):
        at = cols(index, part)
        gate = pre[:, at]
        up = pre[:, pl.ds(pl.multiple_of(hidden + index * part, part), part)]
        hid[:, at] = (gate / (1.0 + jnp.exp(-gate)) * up).astype(jnp.bfloat16)

    @pl.loop(0, n_local)
    def _(block):
        xs_a[:, cols(block)] = jnp.dot(
            hid[...], dn_v[block], preferred_element_type=jnp.float32
        ).astype(jnp.bfloat16)
        give_back(xs_a, back_a, ret_a_send, ret_a_recv, block)

    backward(final)

    @pl.loop(0, n_local)
    def _(block):
        finish_a(block)

    @pl.loop(2 * half - 3, 2 * half)
    def _(turn):
        finish_b(block_at(turn))

    ring_drain(dn)
    ring_drain(gu)

    @pl.loop(0, n_local)
    def _(block):
        all_of(xs_a, ret_a_send.at[block], cols(block)).wait()
        all_of(xs_b, ret_b_send.at[block], cols(block)).wait()

    for slot, (source, target) in enumerate(((res_a, out_a), (res_b, out_b))):
        pltpu.make_async_copy(source, source, relay_send.at[slot]).wait()
        pltpu.make_async_copy(target, target, relay_recv.at[slot]).wait()


def body(
    act_fwd, routes_fwd, weight_fwd, grad_bwd, routes_bwd, weight_bwd, saved_bwd, w_gate_up, w_down
):
    n_node, n_local = lax.axis_size("node"), lax.axis_size("local")
    tokens, features = act_fwd.shape[1:]
    hidden, column = w_down.shape[2:]
    total = n_node * ROWS
    bf16, f32 = jnp.bfloat16, jnp.float32
    anywhere = pl.BlockSpec(memory_space=pl.ANY)
    small = pl.BlockSpec(memory_space=pltpu.VMEM)
    dma = pltpu.SemaphoreType.DMA
    out = jax.ShapeDtypeStruct((tokens, features), bf16)
    next_input, prev_grad = pl.pallas_call(
        kernel,
        out_shape=(out, out),
        in_specs=[anywhere, small, small, anywhere, small, small, anywhere, anywhere, anywhere],
        out_specs=(anywhere, anywhere),
        scratch_shapes=[
            pltpu.VMEM((tokens, features), bf16),
            pltpu.VMEM((tokens, features), bf16),
            pltpu.VMEM((tokens, 2 * hidden), bf16),
            pltpu.VMEM((n_local, column, 2 * hidden), bf16),
            pltpu.VMEM((n_local, hidden, column), bf16),
            pltpu.VMEM((total, features), bf16),
            pltpu.VMEM((total, features), bf16),
            pltpu.VMEM((total, features), bf16),
            pltpu.VMEM((total, features), bf16),
            pltpu.VMEM((total, 2 * hidden), bf16),
            pltpu.VMEM((total, 2 * hidden), bf16),
            pltpu.VMEM((total, features), bf16),
            pltpu.VMEM((total, features), bf16),
            pltpu.VMEM((tokens, features), bf16),
            pltpu.VMEM((tokens, features), bf16),
            pltpu.VMEM((total, 2 * hidden), f32),
            pltpu.VMEM((total, hidden), f32),
            pltpu.VMEM((total, 2 * hidden), bf16),
            pltpu.VMEM((total, hidden), bf16),
            pltpu.VMEM((tokens, total), bf16),
            pltpu.VMEM((tokens, total), bf16),
            pltpu.VMEM((tokens, column), f32),
            dma((5,)), dma((3,)), dma((3,)),
            dma((2 * n_local,)), dma((2 * n_local,)), dma((2 * n_local,)), dma((2 * n_local,)),
            dma((n_local,)), dma((n_local,)), dma((n_local,)), dma((n_local,)),
            dma((2,)), dma((2,)),
        ],
        compiler_params=pltpu.CompilerParams(
            collective_id=0, has_side_effects=True, vmem_limit_bytes=60 * 2**20
        ),
        cost_estimate=pl.CostEstimate(flops=13 * 10**9, bytes_accessed=10 * 2**20, transcendentals=2**19),
    )(
        act_fwd[0],
        routes_fwd.reshape(1, tokens),
        weight_fwd,
        grad_bwd[0],
        routes_bwd.reshape(1, tokens),
        weight_bwd,
        saved_bwd[0],
        w_gate_up[0, 0],
        w_down[0, 0],
    )
    return (next_input[None], prev_grad[None])


def solution(mesh):
    in_specs = (
        P("pp", ("node", "local"), None),
        P("pp", ("node", "local"), None),
        P("pp", ("node", "local")),
        P("pp", ("node", "local"), None),
        P("pp", ("node", "local"), None),
        P("pp", ("node", "local")),
        P("pp", ("node", "local"), None),
        P("pp", "node", "local", None),
        P("pp", "node", None, "local"),
    )
    out_specs = (P("pp", ("node", "local"), None), P("pp", ("node", "local"), None))
    return jax.shard_map(body, mesh=mesh, in_specs=in_specs, out_specs=out_specs, check_vma=False)
```

```python
import functools

import jax
import jax.numpy as jnp
from jax import lax
from jax.experimental import pallas as pl
from jax.experimental.pallas import tpu as pltpu
from jax.sharding import PartitionSpec as P

MESH = pl.DeviceIdType.MESH
NT = (((1,), (1,)), ((), ()))
QUARTERS = 4
PIECES = 4
OFFSETS = (0, 1, -1, 2, -2, 3, -3, 4)


def kernel(
    capacity, act, route_a, weight_a, grad, route_b, weight_b, saved, w_gu, w_dn,
    out_a, out_b,
    act_v, grad_v, saved_v, gu_1, dn_1, gu_v, dn_v, xs_a, xr_a, xq_a, xs_b, xr_b, xq_b, ss, sr, sq,
    back_a, back_b, res_a, res_b, pre, dh, dgu, hid, put, pick_a, pick_b, scale_a, sort, unsort,
    load_sem, disp_send, disp_recv,
    dn_send_1, dn_recv_1, dn_send_2, dn_recv_2, dn_send_3, dn_recv_3, dn_recv_s,
    gu_send_1, gu_recv_1, gu_send_2, gu_recv_2, gu_send_3, gu_recv_3, gu_recv_s,
    ret_a_send, ret_a_recv, ret_b_send, ret_b_recv, relay_send, relay_recv,
):
    n_pp, n_node, n_local = lax.axis_size("pp"), lax.axis_size("node"), lax.axis_size("local")
    pp, node, me = lax.axis_index("pp"), lax.axis_index("node"), lax.axis_index("local")
    tokens, features = act.shape
    hidden, column = w_dn.shape
    slots = QUARTERS * capacity
    total = n_local * slots
    each = n_local * capacity
    width = features // QUARTERS
    piece = width // PIECES

    def wrap(index, size):
        return lax.rem(index + size, size)

    right, left = wrap(node + 2, n_node), wrap(node - 2, n_node)
    sibling = node + 1 - 2 * lax.rem(node, 2)
    ahead, behind = wrap(pp + 1, n_pp), wrap(pp - 1, n_pp)
    peers = [wrap(node + k, n_node) for k in range(1, n_node)]
    planes = [wrap(me + k, n_local) for k in range(1, n_local)]

    def rows_at(index, size):
        return pl.ds(pl.multiple_of(index * size, size), size)

    def send(source, target, send_sem, recv_sem, **to):
        pltpu.make_async_remote_copy(
            src_ref=source, dst_ref=target, send_sem=send_sem, recv_sem=recv_sem,
            device_id=to, device_id_type=MESH,
        ).start()

    def wait(ref, sem):
        pltpu.make_async_copy(ref, ref, sem).wait()

    barrier = pltpu.get_barrier_semaphore()
    for peer in peers:
        pl.semaphore_signal(barrier, inc=1, device_id={"node": peer}, device_id_type=MESH)
    for plane in planes:
        pl.semaphore_signal(barrier, inc=1, device_id={"local": plane}, device_id_type=MESH)
    for neighbour in (behind, ahead):
        pl.semaphore_signal(barrier, inc=1, device_id={"pp": neighbour}, device_id_type=MESH)

    def load(source, target, slot):
        wide = source.shape[1] // QUARTERS
        for q in range(QUARTERS):
            pltpu.make_async_copy(
                source.at[:, pl.ds(q * wide, wide)], target.at[pl.ds(q * tokens, tokens), :],
                load_sem.at[slot],
            ).start()

    load(grad, grad_v, 0)
    load(saved, saved_v, 1)
    load(act, act_v, 2)

    dn = (w_dn, dn_1, dn_v, dn_send_1, dn_recv_1, dn_send_2, dn_recv_2, dn_send_3, dn_recv_3, dn_recv_s)
    gu = (w_gu, gu_1, gu_v, gu_send_1, gu_recv_1, gu_send_2, gu_recv_2, gu_send_3, gu_recv_3, gu_recv_s)

    def step_1_own(array):
        shard, first, _, _, recv_1, *_ = array
        pltpu.make_async_copy(
            shard.at[rows_at(node, first.shape[1]), :], first.at[node], recv_1.at[node]
        ).start()

    def step_1(array):
        shard, first, _, send_1, recv_1, *_ = array
        for peer in peers:
            send(shard.at[rows_at(peer, first.shape[1]), :], first.at[node], send_1.at[0], recv_1.at[node], node=peer)

    def step_2(array):
        _, first, full, _, recv_1, send_2, recv_2, *_ = array
        size = first.shape[1]
        for k in range(n_node):
            expert = wrap(node + k, n_node)
            wait(first.at[expert], recv_1.at[expert])
            target = full.at[me, rows_at(node, size), :]

            @pl.when(expert == me)
            def _():
                pltpu.make_async_copy(first.at[expert], target, recv_2.at[me]).start()

            @pl.when(expert != me)
            def _():
                send(first.at[expert], target, send_2.at[0], recv_2.at[me], local=expert)

    def region(array, block, owner):
        size = array[1].shape[1]
        return array[2].at[block, rows_at(owner, size), :]

    def own_part(array, unit):
        send_3, recv_3, recv_s = array[-3:]
        block = wrap(me + OFFSETS[unit], n_local)
        part = region(array, block, node)
        wait(part, array[6].at[block])
        send(part, part, send_3.at[0], recv_3.at[0, block], node=right)
        send(part, part, send_3.at[1], recv_3.at[1, block], node=left)
        send(part, part, send_3.at[3], recv_s.at[block], node=sibling)

    def next_parts(array, unit):
        send_3, recv_3, recv_s = array[-3:]
        block = wrap(me + OFFSETS[unit], n_local)
        for way, owner in ((0, left), (1, right)):
            part = region(array, block, owner)
            wait(part, recv_3.at[way, block])
            if unit % 2 == way:
                send(part, part, send_3.at[2], recv_3.at[2, block], node=right if way == 0 else left)
            send(part, part, send_3.at[4 + way], recv_s.at[block], node=sibling)

    def last_part(array, unit):
        send_3, recv_3, recv_s = array[-3:]
        block = wrap(me + OFFSETS[unit], n_local)
        part = region(array, block, wrap(node + 4, n_node))
        wait(part, recv_3.at[2, block])
        send(part, part, send_3.at[6], recv_s.at[block], node=sibling)

    def whole(array, block):
        half = array[2].shape[1] // 2
        wait(array[2].at[block, pl.ds(0, half), :], array[-1].at[block])

    def drain(array):
        _, first, full, send_1, _, send_2, _, send_3, *_ = array
        size = first.shape[1]
        wait(first.at[pl.ds(0, n_node - 1)], send_1.at[0])
        wait(full.at[pl.ds(0, n_local - 1), pl.ds(0, size), :], send_2.at[0])
        for kind in range(7):
            wait(full.at[:, pl.ds(0, size), :], send_3.at[kind])

    step_1_own(dn)
    step_1_own(gu)
    pl.semaphore_wait(barrier, n_node - 1 + n_local - 1 + 2)
    step_1(dn)
    step_1(gu)

    def places(route_ref, pick):
        route = jnp.broadcast_to(route_ref[...].astype(jnp.float32), (tokens, tokens))
        turned = jnp.transpose(route)
        first = lax.broadcasted_iota(jnp.int32, (tokens, tokens), 0)
        second = lax.broadcasted_iota(jnp.int32, (tokens, tokens), 1)
        same = route == turned
        slot_row = jnp.sum(jnp.where(same & (first < second), 1.0, 0.0), axis=0, keepdims=True)
        slot_col = jnp.sum(jnp.where(same & (second < first), 1.0, 0.0), axis=1, keepdims=True)
        row = route[0:1, :] * float(slots) + slot_row
        col = turned[:, 0:1] * float(slots) + slot_col
        down = lax.broadcasted_iota(jnp.int32, (total, tokens), 0).astype(jnp.float32)
        along = lax.broadcasted_iota(jnp.int32, (tokens, total), 1).astype(jnp.float32)
        for q in range(QUARTERS):
            shift = float(q * capacity)
            put[:, q * tokens : (q + 1) * tokens] = jnp.where(down == row + shift, 1.0, 0.0).astype(jnp.bfloat16)
            pick[q * tokens : (q + 1) * tokens, :] = jnp.where(along == col + shift, 1.0, 0.0).astype(jnp.bfloat16)

    def spread(weight_ref, wide):
        turned = jnp.transpose(jnp.broadcast_to(weight_ref[...], (tokens, tokens)))
        return jnp.concatenate([turned] * (wide // tokens), axis=1)

    def multiply(left_ref, source, target, wide):
        @pl.loop(0, source.shape[1] // wide)
        def _(index):
            at = rows_at(index, wide)
            target[:, at] = jnp.dot(
                left_ref[...], source[:, at], preferred_element_type=jnp.float32
            ).astype(jnp.bfloat16)

    def dispatch(source, target, slot):
        for plane in planes:
            send(
                source.at[rows_at(plane, slots), :], target.at[rows_at(me, slots), :],
                disp_send.at[slot], disp_recv.at[slot], local=plane,
            )
        target[rows_at(me, slots), :] = source[rows_at(me, slots), :]

    def others(ref, sem, at=slice(None)):
        wait(ref.at[pl.ds(0, total - slots), at], sem)

    places(route_b, pick_b)
    scale_b = spread(weight_b, piece)
    wait(grad_v, load_sem.at[0])
    for q in range(QUARTERS):
        for p in range(PIECES):
            at = (slice(q * tokens, (q + 1) * tokens), slice(p * piece, (p + 1) * piece))
            res_b[at] = (scale_b * grad_v[at].astype(jnp.float32)).astype(jnp.bfloat16)
    multiply(put, res_b, xs_b, 512)
    dispatch(xs_b, xr_b, 0)
    wait(saved_v, load_sem.at[1])
    multiply(put, saved_v, ss, 512)
    dispatch(ss, sr, 1)
    step_2(dn)
    places(route_a, pick_a)
    scale_a[...] = spread(weight_a, piece)
    wait(act_v, load_sem.at[2])
    multiply(put, act_v, xs_a, 512)
    step_2(gu)
    dispatch(xs_a, xr_a, 2)

    def home(index):
        quarter = sum(jnp.where(index >= float(each * j), 1.0, 0.0) for j in range(1, QUARTERS))
        rest = index - quarter * float(each)
        source = sum(jnp.where(rest >= float(capacity * j), 1.0, 0.0) for j in range(1, n_local))
        return source * float(slots) + quarter * float(capacity) + rest - source * float(capacity)

    down = lax.broadcasted_iota(jnp.int32, (total, 128), 0).astype(jnp.float32)
    along = lax.broadcasted_iota(jnp.int32, (8, total), 1).astype(jnp.float32)
    to_col, to_row = home(down)[:, 0:1], home(along)[0:1, :]
    for start in range(0, total, 128):
        across = lax.broadcasted_iota(jnp.int32, (total, 128), 1).astype(jnp.float32) + float(start)
        sort[:, start : start + 128] = jnp.where(across == to_col, 1.0, 0.0).astype(jnp.bfloat16)
        unsort[:, start : start + 128] = jnp.where(down == to_row[:, start : start + 128], 1.0, 0.0).astype(jnp.bfloat16)

    def of_block(block):
        per = width // column
        quarter = lax.div(block, per)
        return rows_at(quarter, each), rows_at(block - quarter * per, column)

    def hidden_grad():
        others(xr_b, disp_recv.at[0])
        multiply(sort, xr_b, xq_b, 512)
        others(sr, disp_recv.at[1])
        multiply(sort, sr, sq, 512)
        dh[...] = jnp.zeros_like(dh)
        for unit in range(n_local):
            whole(dn, wrap(me + OFFSETS[unit], n_local))

        @pl.loop(0, n_local)
        def _(block):
            dh[...] += lax.dot_general(
                xq_b[of_block(block)], dn_v[block], NT, preferred_element_type=jnp.float32
            )

        wide = 2 * hidden // QUARTERS
        for q in range(QUARTERS // 2):
            gate = sq[q * each : (q + 1) * each, :].astype(jnp.float32)
            up = sq[(q + 2) * each : (q + 3) * each, :].astype(jnp.float32)
            grad_h = dh[:, q * wide : (q + 1) * wide]
            sigmoid = 1.0 / (1.0 + jnp.exp(-gate))
            dgu[:, q * wide : (q + 1) * wide] = (
                grad_h * up * sigmoid * (1.0 + gate * (1.0 - sigmoid))
            ).astype(jnp.bfloat16)
            dgu[:, hidden + q * wide : hidden + (q + 1) * wide] = (grad_h * gate * sigmoid).astype(jnp.bfloat16)

    def backward(unit):
        block = wrap(me + OFFSETS[unit], n_local)
        whole(gu, block)
        xq_b[of_block(block)] = lax.dot_general(
            dgu[...], gu_v[block], NT, preferred_element_type=jnp.float32
        ).astype(jnp.bfloat16)

    units = [(array, unit) for array in (dn, gu) for unit in range(n_local)]
    for turn in range(len(units) + 2):
        if turn < len(units):
            own_part(*units[turn])
        if 1 <= turn <= len(units):
            next_parts(*units[turn - 1])
        if turn >= 2:
            last_part(*units[turn - 2])
        if turn == n_local + 2:
            hidden_grad()
        if turn >= n_local + 3:
            backward(turn - n_local - 3)
    backward(n_local - 1)

    def at_piece(p):
        return slice(p * piece, (p + 1) * piece)

    def give_back(sorted_rows, source, target, send_sem, recv_sem, p):
        source[:, at_piece(p)] = jnp.dot(
            unsort[...], sorted_rows[:, at_piece(p)], preferred_element_type=jnp.float32
        ).astype(jnp.bfloat16)
        for plane in planes:
            send(
                source.at[rows_at(plane, slots), at_piece(p)], target.at[rows_at(me, slots), at_piece(p)],
                send_sem.at[p], recv_sem.at[p], local=plane,
            )
        target[rows_at(me, slots), at_piece(p)] = source[rows_at(me, slots), at_piece(p)]

    def relay(source, target, slot, to, p):
        for q in range(QUARTERS):
            send(
                source.at[pl.ds(q * tokens, tokens), at_piece(p)],
                target.at[:, pl.ds(q * width + p * piece, piece)],
                relay_send.at[slot], relay_recv.at[slot], pp=to,
            )

    def finish_b(p):
        others(back_b, ret_b_recv.at[p], at_piece(p))
        moe = jnp.dot(pick_b[...], back_b[:, at_piece(p)], preferred_element_type=jnp.float32)
        res_b[:, at_piece(p)] = (grad_v[:, at_piece(p)].astype(jnp.float32) + moe).astype(jnp.bfloat16)
        relay(res_b, out_b, 1, behind, p)

    def finish_a(p):
        others(back_a, ret_a_recv.at[p], at_piece(p))
        moe = jnp.dot(pick_a[...], back_a[:, at_piece(p)], preferred_element_type=jnp.float32)
        for q in range(QUARTERS):
            at = (slice(q * tokens, (q + 1) * tokens), at_piece(p))
            res_a[at] = (
                act_v[at].astype(jnp.float32) + scale_a[...] * moe[q * tokens : (q + 1) * tokens, :]
            ).astype(jnp.bfloat16)
        relay(res_a, out_a, 0, ahead, p)

    others(xs_b, disp_send.at[0])
    for p in range(PIECES):
        give_back(xq_b, xs_b, back_b, ret_b_send, ret_b_recv, p)

    others(xr_a, disp_recv.at[2])
    multiply(sort, xr_a, xq_a, 512)
    pre[...] = jnp.zeros_like(pre)

    @pl.loop(0, n_local)
    def _(block):
        x = xq_a[of_block(block)]

        @pl.loop(0, 2 * hidden // 512)
        def _(index):
            at = rows_at(index, 512)
            pre[:, at] += jnp.dot(x, gu_v[block, :, at], preferred_element_type=jnp.float32)

    gate = pre[:, :hidden]
    hid[...] = (gate / (1.0 + jnp.exp(-gate)) * pre[:, hidden:]).astype(jnp.bfloat16)
    others(xs_a, disp_send.at[2])
    for p in range(PIECES):
        for q in range(QUARTERS):
            begin = q * width + p * piece
            block, inner = begin // column, begin % column
            xq_a[q * each : (q + 1) * each, at_piece(p)] = jnp.dot(
                hid[...], dn_v[block, :, inner : inner + piece], preferred_element_type=jnp.float32
            ).astype(jnp.bfloat16)
        give_back(xq_a, xs_a, back_a, ret_a_send, ret_a_recv, p)
    for p in range(PIECES):
        finish_b(p)
    for p in range(PIECES):
        finish_a(p)

    drain(dn)
    drain(gu)
    others(ss, disp_send.at[1])
    for p in range(PIECES):
        others(xs_a, ret_a_send.at[p], at_piece(p))
        others(xs_b, ret_b_send.at[p], at_piece(p))
    for slot, (source, target) in enumerate(((res_a, out_a), (res_b, out_b))):
        wait(source, relay_send.at[slot])
        wait(target, relay_recv.at[slot])


def body(
    act_fwd, routes_fwd, weight_fwd, grad_bwd, routes_bwd, weight_bwd, saved_bwd, w_gate_up, w_down
):
    n_node, n_local = lax.axis_size("node"), lax.axis_size("local")
    tokens, features = act_fwd.shape[1:]
    hidden, column = w_down.shape[2:]
    capacity = 5 * tokens // (4 * n_node)
    total = n_local * QUARTERS * capacity
    each = n_local * capacity
    width = features // QUARTERS
    bf16, f32 = jnp.bfloat16, jnp.float32
    anywhere = pl.BlockSpec(memory_space=pl.ANY)
    small = pl.BlockSpec(memory_space=pltpu.VMEM)

    def dma(*shape):
        return pltpu.SemaphoreType.DMA(shape)

    stacked = pltpu.VMEM((QUARTERS * tokens, width), bf16)
    packed = pltpu.VMEM((total, width), bf16)
    packed_saved = pltpu.VMEM((total, 2 * hidden // QUARTERS), bf16)
    of_weights = [dma(1), dma(n_node), dma(1), dma(n_local), dma(7), dma(3, n_local), dma(n_local)]
    out = jax.ShapeDtypeStruct((tokens, features), bf16)
    next_input, prev_grad = pl.pallas_call(
        functools.partial(kernel, capacity),
        out_shape=(out, out),
        in_specs=[anywhere, small, small, anywhere, small, small, anywhere, anywhere, anywhere],
        out_specs=(anywhere, anywhere),
        scratch_shapes=[
            stacked, stacked,
            pltpu.VMEM((QUARTERS * tokens, 2 * hidden // QUARTERS), bf16),
            pltpu.VMEM((n_node, column // n_node, 2 * hidden), bf16),
            pltpu.VMEM((n_node, hidden // n_node, column), bf16),
            pltpu.VMEM((n_local, column, 2 * hidden), bf16),
            pltpu.VMEM((n_local, hidden, column), bf16),
            packed, packed, packed, packed, packed, packed,
            packed_saved, packed_saved, packed_saved,
            packed, packed, stacked, stacked,
            pltpu.VMEM((each, 2 * hidden), f32),
            pltpu.VMEM((each, hidden), f32),
            pltpu.VMEM((each, 2 * hidden), bf16),
            pltpu.VMEM((each, hidden), bf16),
            pltpu.VMEM((total, QUARTERS * tokens), bf16),
            pltpu.VMEM((QUARTERS * tokens, total), bf16),
            pltpu.VMEM((QUARTERS * tokens, total), bf16),
            pltpu.VMEM((tokens, width // PIECES), f32),
            pltpu.VMEM((total, total), bf16),
            pltpu.VMEM((total, total), bf16),
            dma(3), dma(3), dma(3),
            *of_weights, *of_weights,
            dma(PIECES), dma(PIECES), dma(PIECES), dma(PIECES), dma(2), dma(2),
        ],
        compiler_params=pltpu.CompilerParams(
            collective_id=0, has_side_effects=True, vmem_limit_bytes=61 * 2**20
        ),
        cost_estimate=pl.CostEstimate(flops=13 * 10**9, bytes_accessed=10 * 2**20, transcendentals=2**19),
    )(
        act_fwd[0],
        routes_fwd.reshape(1, tokens),
        weight_fwd,
        grad_bwd[0],
        routes_bwd.reshape(1, tokens),
        weight_bwd,
        saved_bwd[0],
        w_gate_up[0, 0],
        w_down[0, 0],
    )
    return (next_input[None], prev_grad[None])


def solution(mesh):
    in_specs = (
        P("pp", ("node", "local"), None),
        P("pp", ("node", "local"), None),
        P("pp", ("node", "local")),
        P("pp", ("node", "local"), None),
        P("pp", ("node", "local"), None),
        P("pp", ("node", "local")),
        P("pp", ("node", "local"), None),
        P("pp", "node", "local", None),
        P("pp", "node", None, "local"),
    )
    out_specs = (P("pp", ("node", "local"), None), P("pp", ("node", "local"), None))
    return jax.shard_map(body, mesh=mesh, in_specs=in_specs, out_specs=out_specs, check_vma=False)
```

```python
import functools

import jax
import jax.numpy as jnp
from jax import lax
from jax.experimental import pallas as pl
from jax.experimental.pallas import tpu as pltpu
from jax.sharding import PartitionSpec as P

MESH = pl.DeviceIdType.MESH
NT = (((1,), (1,)), ((), ()))
QUARTERS = 4
OFFSETS = (0, 2, -2, 4, 1, -1, 3, -3)


def kernel(
    capacity, act, route_a, weight_a, grad, route_b, weight_b, saved, w_gu, w_dn,
    out_a, out_b,
    act_v, grad_v, saved_v, gu_1, dn_1, gu_v, dn_v, xs_a, xr_a, xq_a, xs_b, xr_b, xq_b, ss, sr, sq,
    ys_a, ys_b, back_a, back_b, res_a, res_b, pre, dh, dgu, hid, put, pick_a, pick_b, scale_a, sort, unsort,
    load_sem, disp_send, disp_recv,
    dn_send_1, dn_recv_1, dn_send_2, dn_recv_2, dn_send_3, dn_recv_3, dn_recv_s,
    gu_send_1, gu_recv_1, gu_send_2, gu_recv_2, gu_send_3, gu_recv_3, gu_recv_s,
    ret_a_send, ret_a_recv, ret_b_send, ret_b_recv, relay_send, relay_recv,
):
    n_pp, n_node, n_local = lax.axis_size("pp"), lax.axis_size("node"), lax.axis_size("local")
    pp, node, me = lax.axis_index("pp"), lax.axis_index("node"), lax.axis_index("local")
    tokens, features = act.shape
    hidden, column = w_dn.shape
    slots = QUARTERS * capacity
    total = n_local * slots
    each = n_local * capacity
    width = features // QUARTERS

    def wrap(index, size):
        return lax.rem(index + size, size)

    right, left = wrap(node + 2, n_node), wrap(node - 2, n_node)
    sibling = node + 1 - 2 * lax.rem(node, 2)
    ahead, behind = wrap(pp + 1, n_pp), wrap(pp - 1, n_pp)
    peers = [wrap(node + k, n_node) for k in range(1, n_node)]
    planes = [wrap(me + k, n_local) for k in range(1, n_local)]

    def rows_at(index, size):
        return pl.ds(pl.multiple_of(index * size, size), size)

    def send(source, target, send_sem, recv_sem, **to):
        pltpu.make_async_remote_copy(
            src_ref=source, dst_ref=target, send_sem=send_sem, recv_sem=recv_sem,
            device_id=to, device_id_type=MESH,
        ).start()

    def wait(ref, sem):
        pltpu.make_async_copy(ref, ref, sem).wait()

    barrier = pltpu.get_barrier_semaphore()
    for peer in peers:
        pl.semaphore_signal(barrier, inc=1, device_id={"node": peer}, device_id_type=MESH)
    for plane in planes:
        pl.semaphore_signal(barrier, inc=1, device_id={"local": plane}, device_id_type=MESH)
    for neighbour in (behind, ahead):
        pl.semaphore_signal(barrier, inc=1, device_id={"pp": neighbour}, device_id_type=MESH)

    def load(source, target, slot):
        wide = source.shape[1] // QUARTERS
        for q in range(QUARTERS):
            pltpu.make_async_copy(
                source.at[:, pl.ds(q * wide, wide)], target.at[pl.ds(q * tokens, tokens), :],
                load_sem.at[slot],
            ).start()

    load(grad, grad_v, 0)
    load(saved, saved_v, 1)
    load(act, act_v, 2)

    dn = (w_dn, dn_1, dn_v, dn_send_1, dn_recv_1, dn_send_2, dn_recv_2, dn_send_3, dn_recv_3, dn_recv_s)
    gu = (w_gu, gu_1, gu_v, gu_send_1, gu_recv_1, gu_send_2, gu_recv_2, gu_send_3, gu_recv_3, gu_recv_s)

    def step_1_own(array):
        shard, first, _, _, recv_1, *_ = array
        pltpu.make_async_copy(
            shard.at[rows_at(node, first.shape[1]), :], first.at[node], recv_1.at[node]
        ).start()

    def step_1(array):
        shard, first, _, send_1, recv_1, *_ = array
        for peer in peers:
            send(shard.at[rows_at(peer, first.shape[1]), :], first.at[node], send_1.at[0], recv_1.at[node], node=peer)

    def step_2(array, offsets):
        _, first, full, _, recv_1, send_2, recv_2, *_ = array
        target = full.at[me, rows_at(node, first.shape[1]), :]
        for offset in offsets:
            expert = wrap(me - offset, n_local)
            wait(first.at[expert], recv_1.at[expert])
            if offset == 0:
                pltpu.make_async_copy(first.at[expert], target, recv_2.at[me]).start()
            else:
                send(first.at[expert], target, send_2.at[0], recv_2.at[me], local=expert)

    def region(array, block, owner):
        size = array[1].shape[1]
        return array[2].at[block, rows_at(owner, size), :]

    def own_part(array, unit):
        send_3, recv_3, recv_s = array[-3:]
        block = wrap(me + OFFSETS[unit], n_local)
        part = region(array, block, node)
        wait(part, array[6].at[block])
        send(part, part, send_3.at[0], recv_3.at[0, block], node=right)
        send(part, part, send_3.at[1], recv_3.at[1, block], node=left)
        send(part, part, send_3.at[3], recv_s.at[block], node=sibling)

    def next_parts(array, unit):
        send_3, recv_3, recv_s = array[-3:]
        block = wrap(me + OFFSETS[unit], n_local)
        for way, owner in ((0, left), (1, right)):
            part = region(array, block, owner)
            wait(part, recv_3.at[way, block])
            if unit % 2 == way:
                send(part, part, send_3.at[2], recv_3.at[2, block], node=right if way == 0 else left)
            send(part, part, send_3.at[4 + way], recv_s.at[block], node=sibling)

    def last_part(array, unit):
        send_3, recv_3, recv_s = array[-3:]
        block = wrap(me + OFFSETS[unit], n_local)
        part = region(array, block, wrap(node + 4, n_node))
        wait(part, recv_3.at[2, block])
        send(part, part, send_3.at[6], recv_s.at[block], node=sibling)

    def whole(array, block):
        half = array[2].shape[1] // 2
        wait(array[2].at[block, pl.ds(0, half), :], array[-1].at[block])

    def drain(array):
        _, first, full, send_1, _, send_2, _, send_3, *_ = array
        size = first.shape[1]
        wait(first.at[pl.ds(0, n_node - 1)], send_1.at[0])
        wait(full.at[pl.ds(0, n_local - 1), pl.ds(0, size), :], send_2.at[0])
        for kind in range(7):
            wait(full.at[:, pl.ds(0, size), :], send_3.at[kind])

    step_1_own(dn)
    step_1_own(gu)
    pl.semaphore_wait(barrier, n_node - 1 + n_local - 1 + 2)
    step_1(dn)

    def places(route_ref, pick):
        route = jnp.broadcast_to(route_ref[...].astype(jnp.float32), (tokens, tokens))
        turned = jnp.transpose(route)
        first = lax.broadcasted_iota(jnp.int32, (tokens, tokens), 0)
        second = lax.broadcasted_iota(jnp.int32, (tokens, tokens), 1)
        same = route == turned
        slot_row = jnp.sum(jnp.where(same & (first < second), 1.0, 0.0), axis=0, keepdims=True)
        slot_col = jnp.sum(jnp.where(same & (second < first), 1.0, 0.0), axis=1, keepdims=True)
        row = route[0:1, :] * float(slots) + slot_row
        col = turned[:, 0:1] * float(slots) + slot_col
        down = lax.broadcasted_iota(jnp.int32, (total, tokens), 0).astype(jnp.float32)
        along = lax.broadcasted_iota(jnp.int32, (tokens, total), 1).astype(jnp.float32)
        for q in range(QUARTERS):
            shift = float(q * capacity)
            put[:, q * tokens : (q + 1) * tokens] = jnp.where(down == row + shift, 1.0, 0.0).astype(jnp.bfloat16)
            pick[q * tokens : (q + 1) * tokens, :] = jnp.where(along == col + shift, 1.0, 0.0).astype(jnp.bfloat16)

    def spread(weight_ref, wide):
        turned = jnp.transpose(jnp.broadcast_to(weight_ref[...], (tokens, tokens)))
        return jnp.concatenate([turned] * (wide // tokens), axis=1)

    def multiply(left_ref, source, target, wide):
        @pl.loop(0, source.shape[1] // wide)
        def _(index):
            at = rows_at(index, wide)
            target[:, at] = jnp.dot(
                left_ref[...], source[:, at], preferred_element_type=jnp.float32
            ).astype(jnp.bfloat16)

    def dispatch(source, target, slot, offsets=OFFSETS[1:]):
        for offset in offsets:
            plane = wrap(me - offset, n_local)
            send(
                source.at[rows_at(plane, slots), :], target.at[rows_at(me, slots), :],
                disp_send.at[slot], disp_recv.at[slot], local=plane,
            )

    def keep(source, target):
        target[rows_at(me, slots), :] = source[rows_at(me, slots), :]

    def others(ref, sem, at=slice(None)):
        wait(ref.at[pl.ds(0, total - slots), at], sem)

    places(route_b, pick_b)
    wait(saved_v, load_sem.at[1])
    multiply(put, saved_v, ss, 512)
    dispatch(ss, sr, 1)
    scale_b = spread(weight_b, column)
    scaled = xq_a.at[pl.ds(0, QUARTERS * tokens), :]
    wait(grad_v, load_sem.at[0])
    for q in range(QUARTERS):
        for start in range(0, width, column):
            at = (slice(q * tokens, (q + 1) * tokens), slice(start, start + column))
            scaled[at] = (scale_b * grad_v[at].astype(jnp.float32)).astype(jnp.bfloat16)
    multiply(put, scaled, xs_b, 512)
    step_1(gu)
    step_2(dn, OFFSETS)
    dispatch(xs_b, xr_b, 0)
    keep(ss, sr)
    keep(xs_b, xr_b)
    places(route_a, pick_a)
    scale_a[...] = spread(weight_a, width // QUARTERS)
    wait(act_v, load_sem.at[2])
    multiply(put, act_v, xs_a, 512)
    keep(xs_a, xr_a)

    def home(index):
        quarter = sum(jnp.where(index >= float(each * j), 1.0, 0.0) for j in range(1, QUARTERS))
        rest = index - quarter * float(each)
        source = sum(jnp.where(rest >= float(capacity * j), 1.0, 0.0) for j in range(1, n_local))
        return source * float(slots) + quarter * float(capacity) + rest - source * float(capacity)

    down = lax.broadcasted_iota(jnp.int32, (total, 128), 0).astype(jnp.float32)
    along = lax.broadcasted_iota(jnp.int32, (8, total), 1).astype(jnp.float32)
    to_col, to_row = home(down)[:, 0:1], home(along)[0:1, :]
    for start in range(0, total, 128):
        across = lax.broadcasted_iota(jnp.int32, (total, 128), 1).astype(jnp.float32) + float(start)
        sort[:, start : start + 128] = jnp.where(across == to_col, 1.0, 0.0).astype(jnp.bfloat16)
        unsort[:, start : start + 128] = jnp.where(down == to_row[:, start : start + 128], 1.0, 0.0).astype(jnp.bfloat16)

    def of_block(block):
        per = width // column
        quarter = lax.div(block, per)
        return rows_at(quarter, each), rows_at(block - quarter * per, column)

    def gather_b():
        others(sr, disp_recv.at[1])
        multiply(sort, sr, sq, 512)
        others(xr_b, disp_recv.at[0])
        multiply(sort, xr_b, xq_b, 512)
        dh[...] = jnp.zeros_like(dh)

    def hidden_grad(unit):
        block = wrap(me + OFFSETS[unit], n_local)
        whole(dn, block)
        dh[...] += lax.dot_general(
            xq_b[of_block(block)], dn_v[block], NT, preferred_element_type=jnp.float32
        )

    def gate_up_grad():
        wide = 2 * hidden // QUARTERS
        for q in range(QUARTERS // 2):
            gate = sq[q * each : (q + 1) * each, :].astype(jnp.float32)
            up = sq[(q + 2) * each : (q + 3) * each, :].astype(jnp.float32)
            grad_h = dh[:, q * wide : (q + 1) * wide]
            sigmoid = 1.0 / (1.0 + jnp.exp(-gate))
            dgu[:, q * wide : (q + 1) * wide] = (
                grad_h * up * sigmoid * (1.0 + gate * (1.0 - sigmoid))
            ).astype(jnp.bfloat16)
            dgu[:, hidden + q * wide : hidden + (q + 1) * wide] = (grad_h * gate * sigmoid).astype(jnp.bfloat16)

    def give_back(value, source, target, send_sem, recv_sem, index):
        wide = source.shape[2]
        stacked = jnp.concatenate([value[:, k * wide : (k + 1) * wide] for k in range(QUARTERS)], axis=0)
        source[index] = jnp.dot(unsort[...], stacked, preferred_element_type=jnp.float32).astype(jnp.bfloat16)
        for offset in OFFSETS[1:]:
            plane = wrap(me - offset, n_local)
            send(
                source.at[index, rows_at(plane, slots), :], target.at[index, rows_at(me, slots), :],
                send_sem.at[index], recv_sem.at[index], local=plane,
            )
        target[index, rows_at(me, slots), :] = source[index, rows_at(me, slots), :]

    def backward(unit):
        block = wrap(me + OFFSETS[unit], n_local)
        whole(gu, block)
        value = lax.dot_general(
            dgu[...], gu_v[block], NT, preferred_element_type=jnp.float32
        ).astype(jnp.bfloat16)
        give_back(value, ys_b, back_b, ret_b_send, ret_b_recv, block)

    def gather_a():
        others(xr_a, disp_recv.at[2])
        multiply(sort, xr_a, xq_a, 512)
        pre[...] = jnp.zeros_like(pre)

    def forward(unit):
        block = wrap(me + OFFSETS[unit], n_local)
        x = xq_a[of_block(block)]

        @pl.loop(0, 2 * hidden // 512)
        def _(index):
            at = rows_at(index, 512)
            pre[:, at] += jnp.dot(x, gu_v[block, :, at], preferred_element_type=jnp.float32)

    def moe_rows(index, pick, back, recv_sem):
        wait(back.at[index, pl.ds(0, total - slots), :], recv_sem.at[index])
        return jnp.dot(pick[...], back[index], preferred_element_type=jnp.float32)

    def strips(index, wide):
        per = width // (QUARTERS * wide)
        quarter = lax.div(index, per)
        for k in range(QUARTERS):
            within = (index - quarter * per) * QUARTERS * wide + k * wide
            yield (
                (rows_at(quarter, tokens), pl.ds(pl.multiple_of(within, wide), wide)),
                (slice(None), rows_at(index * QUARTERS + k, wide)),
            )

    def relay(source, target, slot, to, index, wide):
        at = rows_at(index, wide)
        send(source.at[:, at], target.at[:, at], relay_send.at[slot], relay_recv.at[slot], pp=to)

    def finish_b(index):
        moe = moe_rows(index, pick_b, back_b, ret_b_recv)
        wide = back_b.shape[2]
        for k, (stack_at, at) in enumerate(strips(index, wide)):
            res_b[at] = (
                grad_v[stack_at].astype(jnp.float32) + moe[k * tokens : (k + 1) * tokens, :]
            ).astype(jnp.bfloat16)
        relay(res_b, out_b, 1, behind, index, QUARTERS * wide)

    def finish_a(index):
        moe = moe_rows(index, pick_a, back_a, ret_a_recv)
        wide = back_a.shape[2]
        for k, (stack_at, at) in enumerate(strips(index, wide)):
            res_a[at] = (
                act_v[stack_at].astype(jnp.float32) + scale_a[...] * moe[k * tokens : (k + 1) * tokens, :]
            ).astype(jnp.bfloat16)
        relay(res_a, out_a, 0, ahead, index, QUARTERS * wide)

    def finish_b_unit(unit):
        finish_b(wrap(me + OFFSETS[unit], n_local))

    units = [(array, unit) for array in (dn, gu) for unit in range(n_local)]
    extra = {
        2: lambda: step_2(gu, (0, 2, -2)),
        5: lambda: step_2(gu, (4,)),
        6: lambda: dispatch(xs_a, xr_a, 2, (1, -1)),
        7: lambda: step_2(gu, (1, -1)),
        8: lambda: dispatch(xs_a, xr_a, 2, (2, -2)),
        9: lambda: step_2(gu, (3, -3)),
        10: lambda: dispatch(xs_a, xr_a, 2, (3, -3)),
        11: lambda: dispatch(xs_a, xr_a, 2, (4,)),
    }
    for turn in range(len(units) + 4):
        if turn in extra:
            extra[turn]()
        if turn < len(units):
            own_part(*units[turn])
        if 2 <= turn < len(units) + 2:
            next_parts(*units[turn - 2])
        if turn >= 4:
            last_part(*units[turn - 4])
        if turn == 8:
            gather_b()
        if 8 <= turn < 12:
            hidden_grad(2 * turn - 16)
            if turn < 11:
                hidden_grad(2 * turn - 15)
        if turn == 12:
            hidden_grad(n_local - 1)
            gate_up_grad()
        if turn >= 13:
            backward(turn - 13)
        if turn == 17:
            gather_a()
        if turn >= 17:
            forward(2 * turn - 34)
            forward(2 * turn - 33)
    backward(n_local - 1)
    forward(n_local - 2)
    forward(n_local - 1)

    gate = pre[:, :hidden]
    hid[...] = (gate / (1.0 + jnp.exp(-gate)) * pre[:, hidden:]).astype(jnp.bfloat16)
    per = width // column
    for index in range(QUARTERS):
        value = jnp.concatenate(
            [
                jnp.dot(hid[...], dn_v[index * per + k], preferred_element_type=jnp.float32).astype(jnp.bfloat16)
                for k in range(per)
            ],
            axis=1,
        )
        give_back(value, ys_a, back_a, ret_a_send, ret_a_recv, index)
        finish_b_unit(2 * index)
        finish_b_unit(2 * index + 1)
    for index in range(QUARTERS):
        finish_a(index)

    drain(dn)
    drain(gu)
    for slot, source in enumerate((xs_b, ss, xs_a)):
        others(source, disp_send.at[slot])
    for source, sem in ((ys_a, ret_a_send), (ys_b, ret_b_send)):
        for index in range(source.shape[0]):
            wait(source.at[index, pl.ds(0, total - slots), :], sem.at[index])
    for slot, (source, target) in enumerate(((res_a, out_a), (res_b, out_b))):
        wait(source, relay_send.at[slot])
        wait(target, relay_recv.at[slot])


def body(
    act_fwd, routes_fwd, weight_fwd, grad_bwd, routes_bwd, weight_bwd, saved_bwd, w_gate_up, w_down
):
    n_node, n_local = lax.axis_size("node"), lax.axis_size("local")
    tokens, features = act_fwd.shape[1:]
    hidden, column = w_down.shape[2:]
    capacity = 5 * tokens // (4 * n_node)
    total = n_local * QUARTERS * capacity
    each = n_local * capacity
    width = features // QUARTERS
    bf16, f32 = jnp.bfloat16, jnp.float32
    anywhere = pl.BlockSpec(memory_space=pl.ANY)
    small = pl.BlockSpec(memory_space=pltpu.VMEM)

    def dma(*shape):
        return pltpu.SemaphoreType.DMA(shape)

    stacked = pltpu.VMEM((QUARTERS * tokens, width), bf16)
    packed = pltpu.VMEM((total, width), bf16)
    packed_saved = pltpu.VMEM((total, 2 * hidden // QUARTERS), bf16)
    of_weights = [dma(1), dma(n_node), dma(1), dma(n_local), dma(7), dma(3, n_local), dma(n_local)]
    out = jax.ShapeDtypeStruct((tokens, features), bf16)
    next_input, prev_grad = pl.pallas_call(
        functools.partial(kernel, capacity),
        out_shape=(out, out),
        in_specs=[anywhere, small, small, anywhere, small, small, anywhere, anywhere, anywhere],
        out_specs=(anywhere, anywhere),
        scratch_shapes=[
            stacked, stacked,
            pltpu.VMEM((QUARTERS * tokens, 2 * hidden // QUARTERS), bf16),
            pltpu.VMEM((n_node, column // n_node, 2 * hidden), bf16),
            pltpu.VMEM((n_node, hidden // n_node, column), bf16),
            pltpu.VMEM((n_local, column, 2 * hidden), bf16),
            pltpu.VMEM((n_local, hidden, column), bf16),
            packed, packed, packed, packed, packed, packed,
            packed_saved, packed_saved, packed_saved,
            pltpu.VMEM((QUARTERS, total, width // QUARTERS), bf16),
            pltpu.VMEM((n_local, total, column // QUARTERS), bf16),
            pltpu.VMEM((QUARTERS, total, width // QUARTERS), bf16),
            pltpu.VMEM((n_local, total, column // QUARTERS), bf16),
            pltpu.VMEM((tokens, features), bf16),
            pltpu.VMEM((tokens, features), bf16),
            pltpu.VMEM((each, 2 * hidden), f32),
            pltpu.VMEM((each, hidden), f32),
            pltpu.VMEM((each, 2 * hidden), bf16),
            pltpu.VMEM((each, hidden), bf16),
            pltpu.VMEM((total, QUARTERS * tokens), bf16),
            pltpu.VMEM((QUARTERS * tokens, total), bf16),
            pltpu.VMEM((QUARTERS * tokens, total), bf16),
            pltpu.VMEM((tokens, width // QUARTERS), f32),
            pltpu.VMEM((total, total), bf16),
            pltpu.VMEM((total, total), bf16),
            dma(3), dma(3), dma(3),
            *of_weights, *of_weights,
            dma(QUARTERS), dma(QUARTERS), dma(n_local), dma(n_local), dma(2), dma(2),
        ],
        compiler_params=pltpu.CompilerParams(
            collective_id=0, has_side_effects=True, vmem_limit_bytes=61 * 2**20
        ),
        cost_estimate=pl.CostEstimate(flops=13 * 10**9, bytes_accessed=10 * 2**20, transcendentals=2**19),
    )(
        act_fwd[0],
        routes_fwd.reshape(1, tokens),
        weight_fwd,
        grad_bwd[0],
        routes_bwd.reshape(1, tokens),
        weight_bwd,
        saved_bwd[0],
        w_gate_up[0, 0],
        w_down[0, 0],
    )
    return (next_input[None], prev_grad[None])


def solution(mesh):
    in_specs = (
        P("pp", ("node", "local"), None),
        P("pp", ("node", "local"), None),
        P("pp", ("node", "local")),
        P("pp", ("node", "local"), None),
        P("pp", ("node", "local"), None),
        P("pp", ("node", "local")),
        P("pp", ("node", "local"), None),
        P("pp", "node", "local", None),
        P("pp", "node", None, "local"),
    )
    out_specs = (P("pp", ("node", "local"), None), P("pp", ("node", "local"), None))
    return jax.shard_map(body, mesh=mesh, in_specs=in_specs, out_specs=out_specs, check_vma=False)
```

```python
import functools

import jax
import jax.numpy as jnp
from jax import lax
from jax.experimental import pallas as pl
from jax.experimental.pallas import tpu as pltpu
from jax.sharding import PartitionSpec as P

MESH = pl.DeviceIdType.MESH
NT = (((1,), (1,)), ((), ()))
QUARTERS = 4
OFFSETS = (0, 2, -2, 4, 1, -1, 3, -3)


def kernel(
    capacity, act, route_a, weight_a, grad, route_b, weight_b, saved, w_gu, w_dn,
    out_a, out_b,
    act_v, grad_v, saved_v, gu_1, dn_1, gu_v, dn_v, xs_a, xr_a, xq_a, xs_b, xr_b, xq_b, ss, sr, sq,
    ys_a, ys_b, back_a, back_b, res_a, res_b, pre, dh, dgu, hid, put, pick_a, pick_b, scale_a, sort, spare,
    load_sem, disp_send, disp_recv,
    dn_send_1, dn_recv_1, dn_send_2, dn_recv_2, dn_send_3, dn_recv_3, dn_recv_s,
    gu_send_1, gu_recv_1, gu_send_2, gu_recv_2, gu_send_3, gu_recv_3, gu_recv_s,
    ret_a_send, ret_a_recv, ret_b_send, ret_b_recv, relay_send, relay_recv,
):
    n_pp, n_node, n_local = lax.axis_size("pp"), lax.axis_size("node"), lax.axis_size("local")
    pp, node, me = lax.axis_index("pp"), lax.axis_index("node"), lax.axis_index("local")
    tokens, features = act.shape
    hidden, column = w_dn.shape
    slots = QUARTERS * capacity
    total = n_local * slots
    each = n_local * capacity
    width = features // QUARTERS

    def wrap(index, size):
        return lax.rem(index + size, size)

    right, left = wrap(node + 2, n_node), wrap(node - 2, n_node)
    sibling = node + 1 - 2 * lax.rem(node, 2)
    ahead, behind = wrap(pp + 1, n_pp), wrap(pp - 1, n_pp)
    peers = [wrap(node + k, n_node) for k in range(1, n_node)]
    planes = [wrap(me + k, n_local) for k in range(1, n_local)]

    def rows_at(index, size):
        return pl.ds(pl.multiple_of(index * size, size), size)

    def send(source, target, send_sem, recv_sem, **to):
        pltpu.make_async_remote_copy(
            src_ref=source, dst_ref=target, send_sem=send_sem, recv_sem=recv_sem,
            device_id=to, device_id_type=MESH,
        ).start()

    def wait(ref, sem):
        pltpu.make_async_copy(ref, ref, sem).wait()

    barrier = pltpu.get_barrier_semaphore()
    for peer in peers:
        pl.semaphore_signal(barrier, inc=1, device_id={"node": peer}, device_id_type=MESH)
    for plane in planes:
        pl.semaphore_signal(barrier, inc=1, device_id={"local": plane}, device_id_type=MESH)
    for neighbour in (behind, ahead):
        pl.semaphore_signal(barrier, inc=1, device_id={"pp": neighbour}, device_id_type=MESH)

    def load(source, target, slot):
        wide = source.shape[1] // QUARTERS
        for q in range(QUARTERS):
            pltpu.make_async_copy(
                source.at[:, pl.ds(q * wide, wide)], target.at[pl.ds(q * tokens, tokens), :],
                load_sem.at[slot],
            ).start()

    load(grad, grad_v, 0)
    load(saved, saved_v, 1)
    load(act, act_v, 2)

    dn = (w_dn, dn_1, dn_v, dn_send_1, dn_recv_1, dn_send_2, dn_recv_2, dn_send_3, dn_recv_3, dn_recv_s)
    gu = (w_gu, gu_1, gu_v, gu_send_1, gu_recv_1, gu_send_2, gu_recv_2, gu_send_3, gu_recv_3, gu_recv_s)

    def step_1_own(array):
        shard, first, _, _, recv_1, *_ = array
        pltpu.make_async_copy(
            shard.at[rows_at(node, first.shape[1]), :], first.at[node], recv_1.at[node]
        ).start()

    def step_1(array):
        shard, first, _, send_1, recv_1, *_ = array
        for peer in peers:
            send(shard.at[rows_at(peer, first.shape[1]), :], first.at[node], send_1.at[0], recv_1.at[node], node=peer)

    def step_2(array, offsets):
        _, first, full, _, recv_1, send_2, recv_2, *_ = array
        target = full.at[me, rows_at(node, first.shape[1]), :]
        for offset in offsets:
            expert = wrap(me - offset, n_local)
            wait(first.at[expert], recv_1.at[expert])
            if offset == 0:
                pltpu.make_async_copy(first.at[expert], target, recv_2.at[me]).start()
            else:
                send(first.at[expert], target, send_2.at[0], recv_2.at[me], local=expert)

    def region(array, block, owner):
        size = array[1].shape[1]
        return array[2].at[block, rows_at(owner, size), :]

    def own_part(array, unit):
        send_3, recv_3, recv_s = array[-3:]
        block = wrap(me + OFFSETS[unit], n_local)
        part = region(array, block, node)
        wait(part, array[6].at[block])
        send(part, part, send_3.at[0], recv_3.at[0, block], node=right)
        send(part, part, send_3.at[1], recv_3.at[1, block], node=left)
        send(part, part, send_3.at[3], recv_s.at[block], node=sibling)

    def next_parts(array, unit):
        send_3, recv_3, recv_s = array[-3:]
        block = wrap(me + OFFSETS[unit], n_local)
        for way, owner in ((0, left), (1, right)):
            part = region(array, block, owner)
            wait(part, recv_3.at[way, block])
            if unit % 2 == way:
                send(part, part, send_3.at[2], recv_3.at[2, block], node=right if way == 0 else left)
            send(part, part, send_3.at[4 + way], recv_s.at[block], node=sibling)

    def last_part(array, unit):
        send_3, recv_3, recv_s = array[-3:]
        block = wrap(me + OFFSETS[unit], n_local)
        part = region(array, block, wrap(node + 4, n_node))
        wait(part, recv_3.at[2, block])
        send(part, part, send_3.at[6], recv_s.at[block], node=sibling)

    def whole(array, block):
        half = array[2].shape[1] // 2
        wait(array[2].at[block, pl.ds(0, half), :], array[-1].at[block])

    def drain(array):
        _, first, full, send_1, _, send_2, _, send_3, *_ = array
        size = first.shape[1]
        wait(first.at[pl.ds(0, n_node - 1)], send_1.at[0])
        wait(full.at[pl.ds(0, n_local - 1), pl.ds(0, size), :], send_2.at[0])
        for kind in range(7):
            wait(full.at[:, pl.ds(0, size), :], send_3.at[kind])

    step_1_own(dn)
    step_1_own(gu)
    pl.semaphore_wait(barrier, n_node - 1 + n_local - 1 + 2)
    step_1(dn)

    def places(route_ref, pick):
        route = jnp.broadcast_to(route_ref[...].astype(jnp.float32), (tokens, tokens))
        turned = jnp.transpose(route)
        first = lax.broadcasted_iota(jnp.int32, (tokens, tokens), 0)
        second = lax.broadcasted_iota(jnp.int32, (tokens, tokens), 1)
        same = route == turned
        slot_row = jnp.sum(jnp.where(same & (first < second), 1.0, 0.0), axis=0, keepdims=True)
        slot_col = jnp.sum(jnp.where(same & (second < first), 1.0, 0.0), axis=1, keepdims=True)
        row = route[0:1, :] * float(slots) + slot_row
        col = turned[:, 0:1] * float(slots) + slot_col
        down = lax.broadcasted_iota(jnp.int32, (total, tokens), 0).astype(jnp.float32)
        along = lax.broadcasted_iota(jnp.int32, (tokens, total), 1).astype(jnp.float32)
        for q in range(QUARTERS):
            shift = float(q * capacity)
            put[:, q * tokens : (q + 1) * tokens] = jnp.where(down == row + shift, 1.0, 0.0).astype(jnp.bfloat16)
            pick[q * tokens : (q + 1) * tokens, :] = jnp.where(along == col + shift, 1.0, 0.0).astype(jnp.bfloat16)

    def spread(weight_ref, wide):
        turned = jnp.transpose(jnp.broadcast_to(weight_ref[...], (tokens, tokens)))
        return jnp.concatenate([turned] * (wide // tokens), axis=1)

    def multiply(left_ref, source, target, wide):
        @pl.loop(0, source.shape[1] // wide)
        def _(index):
            at = rows_at(index, wide)
            target[:, at] = jnp.dot(
                left_ref[...], source[:, at], preferred_element_type=jnp.float32
            ).astype(jnp.bfloat16)

    def dispatch(source, target, slot, offsets=OFFSETS[1:]):
        for offset in offsets:
            plane = wrap(me - offset, n_local)
            send(
                source.at[rows_at(plane, slots), :], target.at[rows_at(me, slots), :],
                disp_send.at[slot], disp_recv.at[slot], local=plane,
            )

    def keep(source, target):
        target[rows_at(me, slots), :] = source[rows_at(me, slots), :]

    def others(ref, sem, at=slice(None)):
        wait(ref.at[pl.ds(0, total - slots), at], sem)

    places(route_b, pick_b)
    wait(saved_v, load_sem.at[1])
    multiply(put, saved_v, ss, 512)
    dispatch(ss, sr, 1)
    scale_b = spread(weight_b, column)
    scaled = xq_a.at[pl.ds(0, QUARTERS * tokens), :]
    wait(grad_v, load_sem.at[0])
    for q in range(QUARTERS):
        for start in range(0, width, column):
            at = (slice(q * tokens, (q + 1) * tokens), slice(start, start + column))
            scaled[at] = (scale_b * grad_v[at].astype(jnp.float32)).astype(jnp.bfloat16)
    multiply(put, scaled, xs_b, 512)
    step_1(gu)
    step_2(dn, OFFSETS)
    dispatch(xs_b, xr_b, 0)
    keep(ss, sr)
    keep(xs_b, xr_b)
    places(route_a, pick_a)
    scale_a[...] = spread(weight_a, width // QUARTERS)
    wait(act_v, load_sem.at[2])
    multiply(put, act_v, xs_a, 512)
    keep(xs_a, xr_a)

    def home(index):
        quarter = sum(jnp.where(index >= float(each * j), 1.0, 0.0) for j in range(1, QUARTERS))
        rest = index - quarter * float(each)
        source = sum(jnp.where(rest >= float(capacity * j), 1.0, 0.0) for j in range(1, n_local))
        return source * float(slots) + quarter * float(capacity) + rest - source * float(capacity)

    down = lax.broadcasted_iota(jnp.int32, (total, 128), 0).astype(jnp.float32)
    to_col = home(down)[:, 0:1]
    for start in range(0, total, 128):
        across = lax.broadcasted_iota(jnp.int32, (total, 128), 1).astype(jnp.float32) + float(start)
        sort[:, start : start + 128] = jnp.where(across == to_col, 1.0, 0.0).astype(jnp.bfloat16)

    def of_block(block):
        per = width // column
        quarter = lax.div(block, per)
        return rows_at(quarter, each), rows_at(block - quarter * per, column)

    def gather_b():
        others(sr, disp_recv.at[1])
        multiply(sort, sr, sq, 512)
        others(xr_b, disp_recv.at[0])
        multiply(sort, xr_b, xq_b, 512)
        dh[...] = jnp.zeros_like(dh)

    def hidden_grad(unit):
        block = wrap(me + OFFSETS[unit], n_local)
        whole(dn, block)
        dh[...] += lax.dot_general(
            xq_b[of_block(block)], dn_v[block], NT, preferred_element_type=jnp.float32
        )

    def gate_up_grad():
        wide = 2 * hidden // QUARTERS
        for q in range(QUARTERS // 2):
            gate = sq[q * each : (q + 1) * each, :].astype(jnp.float32)
            up = sq[(q + 2) * each : (q + 3) * each, :].astype(jnp.float32)
            grad_h = dh[:, q * wide : (q + 1) * wide]
            sigmoid = 1.0 / (1.0 + jnp.exp(-gate))
            dgu[:, q * wide : (q + 1) * wide] = (
                grad_h * up * sigmoid * (1.0 + gate * (1.0 - sigmoid))
            ).astype(jnp.bfloat16)
            dgu[:, hidden + q * wide : hidden + (q + 1) * wide] = (grad_h * gate * sigmoid).astype(jnp.bfloat16)

    def give_back(value, source, target, send_sem, recv_sem, index):
        wide = source.shape[2]
        for origin in range(n_local):
            for k in range(QUARTERS):
                begin = origin * slots + k * capacity
                spare[begin : begin + capacity, :wide] = value[
                    origin * capacity : (origin + 1) * capacity, k * wide : (k + 1) * wide
                ]
        source[index] = spare[:, :wide].astype(jnp.bfloat16)
        for offset in OFFSETS[1:]:
            plane = wrap(me - offset, n_local)
            send(
                source.at[index, rows_at(plane, slots), :], target.at[index, rows_at(me, slots), :],
                send_sem.at[index], recv_sem.at[index], local=plane,
            )
        target[index, rows_at(me, slots), :] = source[index, rows_at(me, slots), :]

    def backward(unit):
        block = wrap(me + OFFSETS[unit], n_local)
        value = lax.dot_general(dgu[...], gu_v[block], NT, preferred_element_type=jnp.float32)
        give_back(value, ys_b, back_b, ret_b_send, ret_b_recv, block)

    def gather_a():
        others(xr_a, disp_recv.at[2])
        multiply(sort, xr_a, xq_a, 512)
        pre[...] = jnp.zeros_like(pre)

    def forward(unit):
        block = wrap(me + OFFSETS[unit], n_local)
        x = xq_a[of_block(block)]

        @pl.loop(0, 2 * hidden // 512)
        def _(index):
            at = rows_at(index, 512)
            pre[:, at] += jnp.dot(x, gu_v[block, :, at], preferred_element_type=jnp.float32)

    def relay(source, target, slot, to, index):
        at = rows_at(index, width)
        send(source.at[:, at], target.at[:, at], relay_send.at[slot], relay_recv.at[slot], pp=to)

    def strip(index, block, k, wide):
        within = (block * QUARTERS + k) * wide
        return (
            (slice(index * tokens, (index + 1) * tokens), slice(within, within + wide)),
            (slice(None), slice(index * width + within, index * width + within + wide)),
        )

    def finish_b(index):
        per, wide = width // column, back_b.shape[2]
        for block in range(per):
            wait(back_b.at[index * per + block, pl.ds(0, total - slots), :], ret_b_recv.at[index * per + block])
        both = jnp.concatenate([back_b[index * per + block] for block in range(per)], axis=1)
        moe = jnp.dot(pick_b[...], both, preferred_element_type=jnp.float32)
        for block in range(per):
            for k in range(QUARTERS):
                stack_at, at = strip(index, block, k, wide)
                part = moe[k * tokens : (k + 1) * tokens, block * wide : (block + 1) * wide]
                res_b[at] = (grad_v[stack_at].astype(jnp.float32) + part).astype(jnp.bfloat16)
        relay(res_b, out_b, 1, behind, index)

    def finish_a(index):
        wide = back_a.shape[2]
        wait(back_a.at[index, pl.ds(0, total - slots), :], ret_a_recv.at[index])
        moe = jnp.dot(pick_a[...], back_a[index], preferred_element_type=jnp.float32)
        for k in range(QUARTERS):
            stack_at, at = strip(index, 0, k, wide)
            part = moe[k * tokens : (k + 1) * tokens, :]
            res_a[at] = (act_v[stack_at].astype(jnp.float32) + scale_a[...] * part).astype(jnp.bfloat16)
        relay(res_a, out_a, 0, ahead, index)

    units = [(array, unit) for array in (dn, gu) for unit in range(n_local)]
    extra = {
        2: lambda: step_2(gu, (0, 2, -2)),
        5: lambda: step_2(gu, (4,)),
        6: lambda: dispatch(xs_a, xr_a, 2, (1, -1)),
        7: lambda: step_2(gu, (1, -1)),
        8: lambda: dispatch(xs_a, xr_a, 2, (2, -2)),
        9: lambda: step_2(gu, (3, -3)),
        10: lambda: dispatch(xs_a, xr_a, 2, (3, -3)),
        11: lambda: dispatch(xs_a, xr_a, 2, (4,)),
    }
    for turn in range(len(units) + 4):
        if turn in extra:
            extra[turn]()
        if turn < len(units):
            own_part(*units[turn])
        if 2 <= turn < len(units) + 2:
            next_parts(*units[turn - 2])
        if turn >= 4:
            last_part(*units[turn - 4])
        if turn == 8:
            gather_b()
        if 8 <= turn < 12:
            hidden_grad(2 * turn - 16)
            if turn < 11:
                hidden_grad(2 * turn - 15)
        if turn == 12:
            hidden_grad(n_local - 1)
            gate_up_grad()
        if turn >= 13:
            whole(gu, wrap(me + OFFSETS[turn - 13], n_local))
            backward(turn - 13)
        if turn == 17:
            gather_a()
        if turn >= 17:
            forward(2 * turn - 34)
            forward(2 * turn - 33)
    forward(n_local - 2)
    whole(gu, wrap(me + OFFSETS[n_local - 1], n_local))
    forward(n_local - 1)

    gate = pre[:, :hidden]
    hid[...] = (gate / (1.0 + jnp.exp(-gate)) * pre[:, hidden:]).astype(jnp.bfloat16)
    per = width // column
    for index in range(QUARTERS):
        value = jnp.concatenate(
            [
                jnp.dot(hid[...], dn_v[index * per + k], preferred_element_type=jnp.float32)
                for k in range(per)
            ],
            axis=1,
        )
        give_back(value, ys_a, back_a, ret_a_send, ret_a_recv, index)
        if index == 0:
            backward(n_local - 1)
        if index > 0:
            finish_b(index - 1)
    finish_b(QUARTERS - 1)
    for index in range(QUARTERS):
        finish_a(index)

    drain(dn)
    drain(gu)
    for slot, source in enumerate((xs_b, ss, xs_a)):
        others(source, disp_send.at[slot])
    for source, sem in ((ys_a, ret_a_send), (ys_b, ret_b_send)):
        for index in range(source.shape[0]):
            wait(source.at[index, pl.ds(0, total - slots), :], sem.at[index])
    for slot, (source, target) in enumerate(((res_a, out_a), (res_b, out_b))):
        wait(source, relay_send.at[slot])
        wait(target, relay_recv.at[slot])


def body(
    act_fwd, routes_fwd, weight_fwd, grad_bwd, routes_bwd, weight_bwd, saved_bwd, w_gate_up, w_down
):
    n_node, n_local = lax.axis_size("node"), lax.axis_size("local")
    tokens, features = act_fwd.shape[1:]
    hidden, column = w_down.shape[2:]
    capacity = 5 * tokens // (4 * n_node)
    total = n_local * QUARTERS * capacity
    each = n_local * capacity
    width = features // QUARTERS
    bf16, f32 = jnp.bfloat16, jnp.float32
    anywhere = pl.BlockSpec(memory_space=pl.ANY)
    small = pl.BlockSpec(memory_space=pltpu.VMEM)

    def dma(*shape):
        return pltpu.SemaphoreType.DMA(shape)

    stacked = pltpu.VMEM((QUARTERS * tokens, width), bf16)
    packed = pltpu.VMEM((total, width), bf16)
    packed_saved = pltpu.VMEM((total, 2 * hidden // QUARTERS), bf16)
    of_weights = [dma(1), dma(n_node), dma(1), dma(n_local), dma(7), dma(3, n_local), dma(n_local)]
    out = jax.ShapeDtypeStruct((tokens, features), bf16)
    next_input, prev_grad = pl.pallas_call(
        functools.partial(kernel, capacity),
        out_shape=(out, out),
        in_specs=[anywhere, small, small, anywhere, small, small, anywhere, anywhere, anywhere],
        out_specs=(anywhere, anywhere),
        scratch_shapes=[
            stacked, stacked,
            pltpu.VMEM((QUARTERS * tokens, 2 * hidden // QUARTERS), bf16),
            pltpu.VMEM((n_node, column // n_node, 2 * hidden), bf16),
            pltpu.VMEM((n_node, hidden // n_node, column), bf16),
            pltpu.VMEM((n_local, column, 2 * hidden), bf16),
            pltpu.VMEM((n_local, hidden, column), bf16),
            packed, packed, packed, packed, packed, packed,
            packed_saved, packed_saved, packed_saved,
            pltpu.VMEM((QUARTERS, total, width // QUARTERS), bf16),
            pltpu.VMEM((n_local, total, column // QUARTERS), bf16),
            pltpu.VMEM((QUARTERS, total, width // QUARTERS), bf16),
            pltpu.VMEM((n_local, total, column // QUARTERS), bf16),
            pltpu.VMEM((tokens, features), bf16),
            pltpu.VMEM((tokens, features), bf16),
            pltpu.VMEM((each, 2 * hidden), f32),
            pltpu.VMEM((each, hidden), f32),
            pltpu.VMEM((each, 2 * hidden), bf16),
            pltpu.VMEM((each, hidden), bf16),
            pltpu.VMEM((total, QUARTERS * tokens), bf16),
            pltpu.VMEM((QUARTERS * tokens, total), bf16),
            pltpu.VMEM((QUARTERS * tokens, total), bf16),
            pltpu.VMEM((tokens, width // QUARTERS), f32),
            pltpu.VMEM((total, total), bf16),
            pltpu.VMEM((total, width // QUARTERS), f32),
            dma(3), dma(3), dma(3),
            *of_weights, *of_weights,
            dma(QUARTERS), dma(QUARTERS), dma(n_local), dma(n_local), dma(2), dma(2),
        ],
        compiler_params=pltpu.CompilerParams(
            collective_id=0, has_side_effects=True, vmem_limit_bytes=61 * 2**20
        ),
        cost_estimate=pl.CostEstimate(flops=13 * 10**9, bytes_accessed=10 * 2**20, transcendentals=2**19),
    )(
        act_fwd[0],
        routes_fwd.reshape(1, tokens),
        weight_fwd,
        grad_bwd[0],
        routes_bwd.reshape(1, tokens),
        weight_bwd,
        saved_bwd[0],
        w_gate_up[0, 0],
        w_down[0, 0],
    )
    return (next_input[None], prev_grad[None])


def solution(mesh):
    in_specs = (
        P("pp", ("node", "local"), None),
        P("pp", ("node", "local"), None),
        P("pp", ("node", "local")),
        P("pp", ("node", "local"), None),
        P("pp", ("node", "local"), None),
        P("pp", ("node", "local")),
        P("pp", ("node", "local"), None),
        P("pp", "node", "local", None),
        P("pp", "node", None, "local"),
    )
    out_specs = (P("pp", ("node", "local"), None), P("pp", ("node", "local"), None))
    return jax.shard_map(body, mesh=mesh, in_specs=in_specs, out_specs=out_specs, check_vma=False)
```
